32 devices in a mesh: pb: 16 (over z, x, core), ka: 2 (over y).
Axes of the slice: x: 2, y: 2, z: 4, core: 2. Of those that a mesh axis runs over, the one named last changes fastest.
Arguments:
- queries: bfloat16 [4096, 1024], P('pb'), may hold values from -40 to 40
- keys: bfloat16 [4096, 128], P(('ka', 'pb')), may hold values from -20 to 20
- values: bfloat16 [4096, 128], P(('ka', 'pb')), may hold values from -12 to 12
- dout: bfloat16 [4096, 1024], P('pb'), may hold values from -6 to 6
- block_mask: int32 [32, 32], P('pb', 'ka'), may hold values from 0 to 1, as said below
Outputs:
- attended: bfloat16 [4096, 1024], P('pb', 'ka')
- query_grad: float32 [4096, 1024], P('pb', 'ka')
- key_grad: float32 [4096, 128], P(('ka', 'pb'))
- value_grad: float32 [4096, 128], P(('ka', 'pb'))
The draws below stay inside these ranges and needn't reach their ends.
Inputs may be any that keep to these rules, and one draw needn't show every extreme that they name: block_mask[i, j] = 1 lets the 128 queries of block i see the 128 keys of block j. Rows 2 * i and 2 * i + 1 are equal; in both of them the entries of columns 2 * i and 2 * i + 1 are 1, and every aligned run of 16 columns holds at least one 1.
All inputs are finite; a program needn't handle non-finite values.
Results may differ from the reference program's by a relative error of at most 0.017.
Values may be sent and summed in bfloat16 or wider, within the bound.
A program may use at most 64 MiB of HBM per device.

```python
import math
import jax
import jax.numpy as jnp
from jax import lax

HEADS = 8
HEAD_DIM = 128
BLOCK = 128
SEQ = 4096
NBLK = 32
N_KA = 2


def paired_fields(key):
    base_key = jax.random.fold_in(key, 7301)
    keys_q, keys_k, scale_q, scale_k = jax.random.split(base_key, 4)
    key_field = jnp.clip(jax.random.normal(keys_k, (SEQ, HEAD_DIM), jnp.float32), -6.0, 6.0)
    query_field = jnp.clip(jax.random.normal(keys_q, (SEQ, HEADS * HEAD_DIM), jnp.float32), -6.0, 6.0)
    key_field = key_field * jnp.exp(jax.random.uniform(scale_k, (SEQ, 1), jnp.float32, math.log(0.3), math.log(3.0)))
    query_field = query_field * jnp.exp(jax.random.uniform(scale_q, (SEQ, 1), jnp.float32, math.log(0.4), math.log(4.0)))
    return (query_field, key_field)


def draw_queries(key, part):
    return paired_fields(key)[0].astype(jnp.bfloat16)


def draw_keys(key, part):
    return paired_fields(key)[1].astype(jnp.bfloat16)


def draw_block_mask(key, part):
    count = SEQ // BLOCK
    pair_count = count // 2
    panel_blocks = count // N_KA
    roll_key, pick_key = jax.random.split(jax.random.fold_in(key, 4409))
    pair_ids = jnp.arange(pair_count, dtype=jnp.int32)[:, None]
    col_ids = jnp.arange(count, dtype=jnp.int32)[None, :]
    rolls = jax.random.randint(roll_key, (pair_count, count), 0, 100)
    chance = jnp.where(col_ids <= 2 * pair_ids + 1, 85, 15)
    picks = jax.random.randint(pick_key, (pair_count, N_KA), 0, panel_blocks)
    forced = col_ids % panel_blocks == picks[:, col_ids[0] // panel_blocks]
    live = (rolls < chance) | forced | (col_ids // 2 == pair_ids)
    return jnp.repeat(live.astype(jnp.int32), 2, axis=0)


def shard_levels(own_key, shape, cuts, smallest, top_value):
    level = 1.0
    for dim, parts in cuts:
        draws = jax.random.uniform(jax.random.fold_in(jax.random.fold_in(own_key, 6), dim), (parts,), jnp.float32, smallest / len(cuts), top_value / len(cuts))
        level = level * jnp.repeat(jnp.exp(draws), shape[dim] // parts).reshape((-1,) + (1,) * (len(shape) - 1 - dim))
    return level


def centred(key, dims, scale, reach, shards=(), kind=jnp.bfloat16):
    values = scale * jax.random.normal(key, dims, jnp.float32)
    if shards:
        values = values * shard_levels(key, dims, shards, -0.22, 0.18)
    return jnp.clip(values, -reach, reach).astype(kind)


def setup_inputs(seed: int = 0) -> dict:
    streams_of = jax.random.split(jax.random.key(seed), 6)
    queries = draw_queries(jax.random.fold_in(streams_of[5], 71), 0)
    keys = draw_keys(jax.random.fold_in(streams_of[5], 71), 0)
    values = centred(streams_of[2], (SEQ, HEAD_DIM), 2.0, 12.0, ((0, 32),))
    dout = centred(streams_of[3], (SEQ, HEADS * HEAD_DIM), 1.0, 6.0, ((0, 16),))
    block_mask = draw_block_mask(jax.random.fold_in(streams_of[5], 71), 0)
    return {"queries": queries, "keys": keys, "values": values, "dout": dout, "block_mask": block_mask}


def rounded(array_in):
    return lax.optimization_barrier(array_in.astype(jnp.bfloat16)).astype(jnp.float32)

def reference(queries, keys, values, dout, block_mask):
    score_scale = 1.0 / math.sqrt(HEAD_DIM)
    key_rows = SEQ // N_KA
    keys_wide = keys.astype(jnp.float32)
    values_wide = values.astype(jnp.float32)
    key_panels = keys_wide.reshape(N_KA, key_rows, HEAD_DIM)
    value_panels = values_wide.reshape(N_KA, key_rows, HEAD_DIM)
    query_blocks = queries.reshape(NBLK, BLOCK, HEADS, HEAD_DIM)
    dout_blocks = dout.reshape(NBLK, BLOCK, HEADS, HEAD_DIM)

    def one_block(carry, inputs):
        grad_key, grad_value = carry
        query_block, dout_block, mask_row = inputs
        query_wide = query_block.astype(jnp.float32)
        dout_wide = dout_block.astype(jnp.float32)
        live_keys = jnp.repeat(mask_row, BLOCK) > 0
        scores = jnp.einsum('qhd,kd->hqk', query_wide, keys_wide) * score_scale
        panel_scores = scores.reshape(HEADS, BLOCK, N_KA, key_rows)
        panel_live = live_keys.reshape(N_KA, key_rows)
        panel_max = lax.optimization_barrier(jnp.max(jnp.where(panel_live, panel_scores, -jnp.inf), axis=3))
        panel_weights = jnp.where(panel_live, jnp.exp(panel_scores - panel_max[..., None]), 0.0)
        panel_total = lax.optimization_barrier(jnp.sum(panel_weights, axis=3))
        panel_acc = jnp.einsum('hqnk,nkd->hqnd', rounded(panel_weights), value_panels)
        panel_out = rounded(panel_acc / panel_total[..., None])
        panel_lse = panel_max + jnp.log(panel_total)
        row_peak = lax.optimization_barrier(jnp.max(panel_lse, axis=2))
        row_lse = row_peak + jnp.log(lax.optimization_barrier(jnp.sum(jnp.exp(panel_lse - row_peak[..., None]), axis=2)))
        mixing = jnp.exp(panel_lse - row_lse[..., None])
        attended = lax.optimization_barrier(jnp.sum(mixing[..., None] * panel_out, axis=2)).astype(jnp.bfloat16)
        row_delta = lax.optimization_barrier(jnp.sum(dout_wide.transpose(1, 0, 2) * attended.astype(jnp.float32), axis=2))
        probs = jnp.where(live_keys, jnp.exp(scores - row_lse[..., None]), 0.0)
        probs_low = rounded(probs)
        grad_value = grad_value + jnp.einsum('hqk,qhd->kd', probs_low, dout_wide)
        dprobs = jnp.einsum('qhd,kd->hqk', dout_wide, values_wide)
        dscores = rounded(probs * (dprobs - row_delta[..., None]))
        panel_dq = rounded(jnp.einsum('hqnk,nkd->qhnd', dscores.reshape(HEADS, BLOCK, N_KA, key_rows), key_panels) * score_scale)
        grad_query = lax.optimization_barrier(jnp.sum(panel_dq, axis=2))
        grad_key = grad_key + jnp.einsum('hqk,qhd->kd', dscores, query_wide) * score_scale
        out_rows = attended.transpose(1, 0, 2).reshape(BLOCK, HEADS * HEAD_DIM)
        return ((grad_key, grad_value), (out_rows, grad_query.reshape(BLOCK, HEADS * HEAD_DIM)))
    start = (jnp.zeros((SEQ, HEAD_DIM), jnp.float32), jnp.zeros((SEQ, HEAD_DIM), jnp.float32))
    (grad_key, grad_value), (attended, grad_query) = lax.scan(one_block, start, (query_blocks, dout_blocks, block_mask))
    return (attended.reshape(SEQ, HEADS * HEAD_DIM), grad_query.reshape(SEQ, HEADS * HEAD_DIM), grad_key, grad_value)
```

```python
import functools
import math

import jax
import jax.numpy as jnp
from jax import lax
from jax.experimental import pallas as pl
from jax.experimental.pallas import tpu as pltpu
from jax.sharding import PartitionSpec as P

BLOCK = 128
DEAD = 1e30
F32 = jnp.float32
BF16 = jnp.bfloat16


def dot_nn(a, b):
    return jnp.dot(a, b, preferred_element_type=F32)


def dot_nt(a, b):
    return lax.dot_general(a, b, (((1,), (1,)), ((), ())), preferred_element_type=F32)


def kernel(
    n_pb, n_ka,
    mask_ref, q_ref, k_ref, v_ref, do_ref,
    att_ref, qg_ref, kg_ref, vg_ref,
    kv, k_turned, q_turned, do_turned, q_scaled, do_scaled, weights, dscores,
    out_acc, dq_acc, run_max, run_total, group_max, row_lse, row_delta,
    stat_recv, out_send, out_recv, dq_send, dq_recv,
    acc, core_send, core_recv, x_send, x_recv, z_send, z_recv,
    ag_recv_sem, ag_z_sem, ag_x_sem, ag_core_sem,
    stat_send_sem, stat_recv_sem, out_send_sem, out_recv_sem, dq_send_sem, dq_recv_sem,
    core_send_sem, core_recv_sem, x_send_sem, x_recv_sem, z_send_sem, z_recv_sem,
):
    rows, width = q_ref.shape
    chunk, dim = k_ref.shape
    heads = width // dim
    own_heads = heads // n_ka
    groups = n_pb // 4
    group_keys = 4 * chunk
    group_blocks = group_keys // BLOCK
    scale = 1.0 / math.sqrt(dim)
    log_scale = scale * math.log2(math.e)

    me = lax.axis_index("pb")
    panel = lax.axis_index("ka")
    core = lax.rem(me, 2)
    x = lax.rem(me // 2, 2)
    z = me // 4
    other_core, other_x = 1 - core, 1 - x

    def at(z_index, x_index, core_index):
        return (z_index * 2 + x_index) * 2 + core_index

    core_peer, x_peer = at(z, x, other_core), at(z, other_x, core)

    def remote(src, dst, send_sem, recv_sem, device):
        return pltpu.make_async_remote_copy(
            src_ref=src, dst_ref=dst, send_sem=send_sem, recv_sem=recv_sem,
            device_id=device, device_id_type=pl.DeviceIdType.MESH,
        )

    def ring(start, step, size):
        return lax.rem(start + step, size)

    barrier = pltpu.get_barrier_semaphore()
    partners = [{"pb": core_peer}, {"pb": x_peer}]
    partners += [{"pb": at(ring(z, s, groups), x, core)} for s in range(1, groups)]
    partners += [{"ka": ring(panel, s, n_ka)} for s in range(1, n_ka)]
    for partner in partners:
        pl.semaphore_signal(barrier, inc=1, device_id=partner, device_id_type=pl.DeviceIdType.MESH)
    kv[me, 0:chunk, :] = k_ref[...]
    kv[me, chunk : 2 * chunk, :] = v_ref[...]
    pl.semaphore_wait(barrier, len(partners))

    def gather_copy(index, send_sem, device):
        return remote(kv.at[index], kv.at[index], send_sem, ag_recv_sem.at[index], {"pb": device})

    def z_copy(s):
        return gather_copy(me, ag_z_sem.at[s], at(ring(z, s, groups), x, core))

    def x_copy(k):
        return gather_copy(at(ring(z, k, groups), x, core), ag_x_sem.at[k], x_peer)

    def core_copy(k, part):
        owner_x = x if part == 0 else other_x
        index = at(ring(z, k, groups), owner_x, core)
        return gather_copy(index, ag_core_sem.at[2 * k + part], core_peer)

    def arrived(index):
        gather_copy(index, ag_x_sem.at[0], core_peer).wait_recv()

    x_copy(0).start()
    core_copy(0, 0).start()
    for s in range(1, groups):
        z_copy(s).start()

    def head_columns(head):
        return pl.ds(pl.multiple_of(head * rows, rows), rows)

    def head_at(i):
        return lax.rem((panel + 1) * own_heads + i, heads)

    for head in range(heads):
        source = pl.ds(head * dim, dim)
        target = pl.ds(head * rows, rows)
        q_turned[:, target] = q_ref[:, source].T
        do_turned[:, target] = do_ref[:, source].T
    out_acc[...] = jnp.zeros_like(out_acc)
    dq_acc[...] = jnp.zeros_like(dq_acc)
    run_max[...] = jnp.full_like(run_max, -1e38)
    run_total[...] = jnp.zeros_like(run_total)

    def stage_x(k):
        arrived(at(ring(z, k, groups), other_x, core))
        core_copy(k, 1).start()

    def stage_core(k):
        arrived(at(ring(z, k, groups), x, other_core))
        arrived(at(ring(z, k, groups), other_x, other_core))

    stage_x(0)
    stage_core(0)

    def group_rows(group, first):
        return kv[pl.ds(group * 4, 4), first : first + chunk, :].reshape(group_keys, dim)

    def forward_group(k, _):
        group = ring(z, k, groups)
        more = k < groups - 1

        @pl.when(more)
        def _():
            arrived(at(ring(z, k + 1, groups), x, core))
            x_copy(k + 1).start()
            core_copy(k + 1, 0).start()

        keys = group_rows(group, 0)
        k_turned[group] = keys.T
        values_turned = group_rows(group, chunk).T
        bias = [
            (mask_ref[0, group * group_blocks + b].astype(F32) - 1.0) * DEAD
            for b in range(group_blocks)
        ]

        def forward_head(i, _):
            cols = head_columns(head_at(i))
            scores = dot_nn(group_rows(group, 0), q_turned[:, cols])
            parts = [
                scores[b * BLOCK : (b + 1) * BLOCK] * log_scale + bias[b]
                for b in range(group_blocks)
            ]
            peak = functools.reduce(
                jnp.maximum, [jnp.max(part, axis=0, keepdims=True) for part in parts]
            )
            low = []
            total = jnp.zeros_like(peak)
            for part in parts:
                weight = jnp.exp2(part - peak)
                total = total + jnp.sum(weight, axis=0, keepdims=True)
                low.append(weight.astype(BF16))
            low = jnp.concatenate(low, axis=0)
            weights[group, :, cols] = low
            group_max[group, :, cols] = peak
            old = run_max[:, cols]
            new = jnp.maximum(old, peak)
            keep, add = jnp.exp2(old - new), jnp.exp2(peak - new)
            run_max[:, cols] = new
            run_total[:, cols] = run_total[:, cols] * keep + total * add
            out_acc[:, cols] = out_acc[:, cols] * keep + dot_nn(values_turned, low) * add
            return 0

        lax.fori_loop(0, heads // 2, forward_head, 0, unroll=2)

        @pl.when(more)
        def _():
            stage_x(k + 1)

        lax.fori_loop(heads // 2, heads, forward_head, 0, unroll=2)

        @pl.when(more)
        def _():
            stage_core(k + 1)

        return 0

    lax.fori_loop(0, groups, forward_group, 0)

    def stat_copy(head, s):
        return remote(
            stat_recv.at[panel, head], stat_recv.at[panel, head],
            stat_send_sem.at[head, s], stat_recv_sem.at[panel, head],
            {"ka": ring(panel, s, n_ka)},
        )

    def stat_arrived(head, source):
        remote(
            stat_recv.at[source, head], stat_recv.at[source, head],
            stat_send_sem.at[head, 0], stat_recv_sem.at[source, head],
            {"ka": ring(panel, 1, n_ka)},
        ).wait_recv()

    def part_copy(send, recv, send_sem, recv_sem, head):
        local = lax.rem(head, own_heads)
        return remote(
            send.at[head], recv.at[panel, local], send_sem.at[head], recv_sem.at[panel, local],
            {"ka": head // own_heads},
        )

    def part_arrived(recv, send_sem, recv_sem, source, local):
        remote(
            recv.at[source, local], recv.at[source, local],
            send_sem.at[0], recv_sem.at[source, local], {"ka": ring(panel, 1, n_ka)},
        ).wait_recv()

    def finish_head(i, _):
        head = head_at(i)
        cols = head_columns(head)
        total = run_total[:, cols]
        out = out_acc[:, cols] * (1.0 / total)
        delta = jnp.sum(out * do_turned[:, cols].astype(F32), axis=0, keepdims=True)
        stat_recv[panel, head, 0:1, :] = run_max[:, cols] + jnp.log2(total)
        stat_recv[panel, head, 1:2, :] = delta
        for s in range(1, n_ka):
            stat_copy(head, s).start()

        @pl.when(i < heads - own_heads)
        def _():
            out_send[head] = out.astype(BF16)
            part_copy(out_send, out_recv, out_send_sem, out_recv_sem, head).start()

        @pl.when(i >= heads - own_heads)
        def _():
            out_recv[panel, lax.rem(head, own_heads)] = out.astype(BF16)

        return 0

    lax.fori_loop(0, heads, finish_head, 0)

    def merge_head(i, _):
        head = head_at(i)
        cols = head_columns(head)
        for s in range(1, n_ka):
            stat_arrived(head, ring(panel, s, n_ka))
        lses = [stat_recv[n, head, 0:1, :] for n in range(n_ka)]
        peak = functools.reduce(jnp.maximum, lses)
        lse = peak + jnp.log2(sum(jnp.exp2(one - peak) for one in lses))
        row_lse[:, cols] = lse
        row_delta[:, cols] = sum(
            jnp.exp2(lses[n] - lse) * stat_recv[n, head, 1:2, :] for n in range(n_ka)
        )
        return 0

    lax.fori_loop(0, heads, merge_head, 0)

    def back_group_of(k):
        return ring(z, k + 1, groups)

    def core_sum_copy(k):
        return remote(
            core_send.at[k], core_recv.at[k], core_send_sem.at[k], core_recv_sem.at[k],
            {"pb": core_peer},
        )

    def x_sum_copy(k):
        return remote(
            x_send.at[k], x_recv.at[k], x_send_sem.at[k], x_recv_sem.at[k], {"pb": x_peer}
        )

    def z_sum_copy(k):
        return remote(
            z_send.at[k], z_recv.at[k], z_send_sem.at[k], z_recv_sem.at[k],
            {"pb": at(back_group_of(k), x, core)},
        )

    def send_core(k):
        slot = lax.rem(k, 2)
        for part in range(2):
            core_send[k, part] = acc[slot, 2 * part + other_core].astype(BF16)
        core_sum_copy(k).start()

    def send_x(k):
        slot = lax.rem(k, 2)
        core_sum_copy(k).wait_recv()
        passed = acc[slot, 2 * other_x + core] + core_recv[k, other_x].astype(F32)
        x_send[k] = passed.astype(BF16)
        x_sum_copy(k).start()
        mine = 2 * x + core
        acc[slot, mine] = acc[slot, mine] + core_recv[k, x].astype(F32)

    def x_total(k):
        x_sum_copy(k).wait_recv()
        return acc[lax.rem(k, 2), 2 * x + core] + x_recv[k].astype(F32)

    def send_z(k):
        z_send[k] = x_total(k).astype(BF16)
        z_sum_copy(k).start()

    def backward_group(k, _):
        group = back_group_of(k)
        slot = lax.rem(k, 2)

        def backward_head(i, _):
            head = head_at(i)
            cols = head_columns(head)
            mix = jnp.exp2(group_max[group, :, cols] - row_lse[:, cols])
            dprobs = dot_nn(group_rows(group, chunk), do_turned[:, cols])
            ds = weights[group, :, cols] * (dprobs - row_delta[:, cols]).astype(BF16)
            dscores[:, cols] = ds
            q_scaled[:, cols] = (q_turned[:, cols].astype(F32) * (mix * scale)).astype(BF16)
            do_scaled[:, cols] = (do_turned[:, cols].astype(F32) * mix).astype(BF16)
            dq_acc[:, cols] = dq_acc[:, cols] + dot_nn(k_turned[group], ds) * (mix * scale)

            @pl.when((k == groups - 1) & (i < heads - own_heads))
            def _():
                dq_send[head] = dq_acc[:, cols].astype(BF16)
                part_copy(dq_send, dq_recv, dq_send_sem, dq_recv_sem, head).start()

            return 0

        lax.fori_loop(0, heads // 2, backward_head, 0, unroll=2)

        @pl.when(k > 0)
        def _():
            send_x(k - 1)

        lax.fori_loop(heads // 2, heads, backward_head, 0, unroll=2)

        @pl.when(k > 0)
        def _():
            send_z(k - 1)

        key_part = dot_nt(dscores[...], q_scaled[...])
        value_part = dot_nt(weights[group], do_scaled[...])
        acc[slot, :, 0:chunk, :] = key_part.reshape(4, chunk, dim)
        acc[slot, :, chunk : 2 * chunk, :] = value_part.reshape(4, chunk, dim)
        send_core(k)
        return 0

    lax.fori_loop(0, groups, backward_group, 0)

    for local in range(own_heads):
        head = panel * own_heads + local
        cols = head_columns(head)
        for s in range(1, n_ka):
            part_arrived(out_recv, out_send_sem, out_recv_sem, ring(panel, s, n_ka), local)
        lse = row_lse[:, cols]
        mixed = sum(
            jnp.exp2(stat_recv[n, head, 0:1, :] - lse) * out_recv[n, local].astype(F32)
            for n in range(n_ka)
        )
        att_ref[:, local * dim : (local + 1) * dim] = mixed.T.astype(BF16)
        dq_recv[panel, local] = dq_acc[:, cols].astype(BF16)

    last = groups - 1
    send_x(last)
    total = x_total(last)
    for k in range(last):
        z_sum_copy(k).wait_recv()
        total = total + z_recv[k].astype(F32)
    kg_ref[...] = total[0:chunk]
    vg_ref[...] = total[chunk : 2 * chunk]

    for local in range(own_heads):
        for s in range(1, n_ka):
            part_arrived(dq_recv, dq_send_sem, dq_recv_sem, ring(panel, s, n_ka), local)
        summed = sum(dq_recv[n, local].astype(F32) for n in range(n_ka))
        qg_ref[:, local * dim : (local + 1) * dim] = summed.T

    def drain_group(k, _):
        x_copy(k).wait_send()
        core_copy(k, 0).wait_send()
        core_copy(k, 1).wait_send()
        core_sum_copy(k).wait_send()
        x_sum_copy(k).wait_send()

        @pl.when(k < last)
        def _():
            z_copy(k + 1).wait_send()
            z_sum_copy(k).wait_send()

        return 0

    lax.fori_loop(0, groups, drain_group, 0)

    def drain_head(i, _):
        head = head_at(i)
        for s in range(1, n_ka):
            stat_copy(head, s).wait_send()

        @pl.when(i < heads - own_heads)
        def _():
            part_copy(out_send, out_recv, out_send_sem, out_recv_sem, head).wait_send()
            part_copy(dq_send, dq_recv, dq_send_sem, dq_recv_sem, head).wait_send()

        return 0

    lax.fori_loop(0, heads, drain_head, 0)


def per_device(n_pb, n_ka, queries, keys, values, dout, block_mask):
    rows, width = queries.shape
    chunk, dim = keys.shape
    heads = width // dim
    own_heads = heads // n_ka
    groups = n_pb // 4
    group_keys = 4 * chunk
    wide = heads * rows
    assert rows == 2 * BLOCK and group_keys % BLOCK == 0
    vmem, dma = pltpu.VMEM, pltpu.SemaphoreType.DMA
    pair = (2 * chunk, dim)
    return pl.pallas_call(
        functools.partial(kernel, n_pb, n_ka),
        out_shape=(
            jax.ShapeDtypeStruct((rows, own_heads * dim), BF16),
            jax.ShapeDtypeStruct((rows, own_heads * dim), F32),
            jax.ShapeDtypeStruct((chunk, dim), F32),
            jax.ShapeDtypeStruct((chunk, dim), F32),
        ),
        in_specs=[pl.BlockSpec(memory_space=pltpu.SMEM)]
        + [pl.BlockSpec(memory_space=pltpu.VMEM)] * 4,
        out_specs=[pl.BlockSpec(memory_space=pltpu.VMEM)] * 4,
        scratch_shapes=[
            vmem((n_pb,) + pair, BF16),
            vmem((groups, dim, group_keys), BF16),
            vmem((dim, wide), BF16),
            vmem((dim, wide), BF16),
            vmem((dim, wide), BF16),
            vmem((dim, wide), BF16),
            vmem((groups, group_keys, wide), BF16),
            vmem((group_keys, wide), BF16),
            vmem((dim, wide), F32),
            vmem((dim, wide), F32),
            vmem((1, wide), F32),
            vmem((1, wide), F32),
            vmem((groups, 1, wide), F32),
            vmem((1, wide), F32),
            vmem((1, wide), F32),
            vmem((n_ka, heads, 8, rows), F32),
            vmem((heads, dim, rows), BF16),
            vmem((n_ka, own_heads, dim, rows), BF16),
            vmem((heads, dim, rows), BF16),
            vmem((n_ka, own_heads, dim, rows), BF16),
            vmem((2, 4) + pair, F32),
            vmem((groups, 2) + pair, BF16),
            vmem((groups, 2) + pair, BF16),
            vmem((groups,) + pair, BF16),
            vmem((groups,) + pair, BF16),
            vmem((groups,) + pair, BF16),
            vmem((groups,) + pair, BF16),
            dma((n_pb,)),
            dma((groups,)),
            dma((groups,)),
            dma((2 * groups,)),
            dma((heads, n_ka)),
            dma((n_ka, heads)),
            dma((heads,)),
            dma((n_ka, own_heads)),
            dma((heads,)),
            dma((n_ka, own_heads)),
            dma((groups,)),
            dma((groups,)),
            dma((groups,)),
            dma((groups,)),
            dma((groups,)),
            dma((groups,)),
        ],
        compiler_params=pltpu.CompilerParams(
            collective_id=0, has_side_effects=True, vmem_limit_bytes=52 * 2**20
        ),
        cost_estimate=pl.CostEstimate(
            flops=12 * wide * n_pb * chunk * dim,
            bytes_accessed=4 * rows * width * 2,
            transcendentals=wide * n_pb * chunk,
        ),
    )(block_mask, queries, keys, values, dout)


def solution(mesh):
    in_specs = (
        P("pb", None),
        P(("ka", "pb"), None),
        P(("ka", "pb"), None),
        P("pb", None),
        P("pb", "ka"),
    )
    out_specs = (P("pb", "ka"), P("pb", "ka"), P(("ka", "pb"), None), P(("ka", "pb"), None))
    return jax.shard_map(
        functools.partial(per_device, mesh.shape["pb"], mesh.shape["ka"]),
        mesh=mesh, in_specs=in_specs, out_specs=out_specs, check_vma=False,
    )
```

```python
import functools
import math

import jax
import jax.numpy as jnp
from jax import lax
from jax.experimental import pallas as pl
from jax.experimental.pallas import tpu as pltpu
from jax.sharding import PartitionSpec as P

BLOCK = 128
DEAD = 1e30
F32 = jnp.float32
BF16 = jnp.bfloat16


def dot_nn(a, b):
    return jnp.dot(a, b, preferred_element_type=F32)


def dot_nt(a, b):
    return lax.dot_general(a, b, (((1,), (1,)), ((), ())), preferred_element_type=F32)


def kernel(
    n_pb, n_ka,
    mask_ref, q_ref, k_ref, v_ref, do_ref,
    att_ref, qg_ref, kg_ref, vg_ref,
    kv, k_turned, q_rows, do_rows, q_turned, do_turned, weights, wide_scores, probs, dscores,
    out_acc, dq_acc, run_max, run_total, group_max, row_lse, row_delta,
    stat_recv, out_send, out_recv, dq_send, dq_recv,
    acc, core_send, core_recv, x_send, x_recv, z_send, z_recv,
    load_sem, ag_recv_sem, ag_z_sem, ag_x_sem, ag_core_sem,
    stat_send_sem, stat_recv_sem, out_send_sem, out_recv_sem, dq_send_sem, dq_recv_sem,
    core_send_sem, core_recv_sem, x_send_sem, x_recv_sem, z_send_sem, z_recv_sem,
):
    rows, width = q_ref.shape
    chunk, dim = k_ref.shape
    heads = width // dim
    own_heads = heads // n_ka
    groups = n_pb // 4
    group_keys = 4 * chunk
    group_blocks = group_keys // BLOCK
    scale = 1.0 / math.sqrt(dim)
    log_scale = scale * math.log2(math.e)

    me = lax.axis_index("pb")
    panel = lax.axis_index("ka")
    core = lax.rem(me, 2)
    x = lax.rem(me // 2, 2)
    z = me // 4
    other_core, other_x = 1 - core, 1 - x

    def at(z_index, x_index, core_index):
        return (z_index * 2 + x_index) * 2 + core_index

    core_peer, x_peer = at(z, x, other_core), at(z, other_x, core)

    def remote(src, dst, send_sem, recv_sem, device):
        return pltpu.make_async_remote_copy(
            src_ref=src, dst_ref=dst, send_sem=send_sem, recv_sem=recv_sem,
            device_id=device, device_id_type=pl.DeviceIdType.MESH,
        )

    def ring(start, step, size):
        return lax.rem(start + step, size)

    def load(index, src, dst):
        return pltpu.make_async_copy(src, dst, load_sem.at[index])

    loads = [
        load(0, k_ref, kv.at[me, pl.ds(0, chunk)]),
        load(1, v_ref, kv.at[me, pl.ds(chunk, chunk)]),
    ]
    for part, (src, dst) in enumerate(((q_ref, q_rows), (do_ref, do_rows))):
        for head in range(heads):
            loads.append(
                load(
                    2 + part * heads + head,
                    src.at[:, pl.ds(head * dim, dim)],
                    dst.at[pl.ds(head * rows, rows), :],
                )
            )
    for one in loads:
        one.start()

    barrier = pltpu.get_barrier_semaphore()
    partners = [{"pb": core_peer}, {"pb": x_peer}]
    partners += [{"pb": at(ring(z, s, groups), x, core)} for s in range(1, groups)]
    partners += [{"ka": ring(panel, s, n_ka)} for s in range(1, n_ka)]
    for partner in partners:
        pl.semaphore_signal(barrier, inc=1, device_id=partner, device_id_type=pl.DeviceIdType.MESH)
    loads[0].wait()
    loads[1].wait()
    pl.semaphore_wait(barrier, len(partners))

    def gather_copy(index, send_sem, device):
        return remote(kv.at[index], kv.at[index], send_sem, ag_recv_sem.at[index], {"pb": device})

    def z_copy(s):
        return gather_copy(me, ag_z_sem.at[s], at(ring(z, s, groups), x, core))

    def x_copy(k):
        return gather_copy(at(ring(z, k, groups), x, core), ag_x_sem.at[k], x_peer)

    def core_copy(k, part):
        owner_x = x if part == 0 else other_x
        index = at(ring(z, k, groups), owner_x, core)
        return gather_copy(index, ag_core_sem.at[2 * k + part], core_peer)

    def arrived(index):
        gather_copy(index, ag_x_sem.at[0], core_peer).wait_recv()

    x_copy(0).start()
    core_copy(0, 0).start()
    for s in range(1, groups):
        z_copy(s).start()

    def head_columns(head):
        return pl.ds(pl.multiple_of(head * rows, rows), rows)

    def head_at(i):
        return lax.rem((panel + 1) * own_heads + i, heads)

    for one in loads[2:]:
        one.wait()
    for head in range(heads):
        span = pl.ds(head * rows, rows)
        q_turned[:, span] = q_rows[span, :].T
        do_turned[:, span] = do_rows[span, :].T
    out_acc[...] = jnp.zeros_like(out_acc)
    dq_acc[...] = jnp.zeros_like(dq_acc)
    run_max[...] = jnp.full_like(run_max, -1e38)
    run_total[...] = jnp.zeros_like(run_total)

    def stage_x(k):
        arrived(at(ring(z, k, groups), other_x, core))
        core_copy(k, 1).start()

    def stage_core(k):
        arrived(at(ring(z, k, groups), x, other_core))
        arrived(at(ring(z, k, groups), other_x, other_core))

    stage_x(0)
    stage_core(0)

    def group_rows(group, first):
        return kv[pl.ds(group * 4, 4), first : first + chunk, :].reshape(group_keys, dim)

    def forward_group(k, _):
        group = ring(z, k, groups)
        more = k < groups - 1

        @pl.when(more)
        def _():
            arrived(at(ring(z, k + 1, groups), x, core))
            x_copy(k + 1).start()
            core_copy(k + 1, 0).start()

        keys = group_rows(group, 0)
        k_turned[group] = keys.T
        values_turned = group_rows(group, chunk).T
        bias = [
            (mask_ref[0, group * group_blocks + b].astype(F32) - 1.0) * DEAD
            for b in range(group_blocks)
        ]

        def forward_heads(first, last):
            def score(i):
                scores = dot_nn(group_rows(group, 0), q_turned[:, head_columns(head_at(i))])
                wide_scores[i - first] = scores
                return [
                    jnp.max(scores[b * BLOCK : (b + 1) * BLOCK], axis=0, keepdims=True) * log_scale
                    for b in range(group_blocks)
                ]

            peaks = score(first)
            for i in range(first, last):
                later = score(i + 1) if i + 1 < last else None
                cols = head_columns(head_at(i))
                peak = functools.reduce(jnp.maximum, [p + one for p, one in zip(peaks, bias)])
                low = []
                total = jnp.zeros_like(peak)
                for b in range(group_blocks):
                    shift = jnp.maximum(peak - bias[b], peaks[b])
                    part = wide_scores[i - first, b * BLOCK : (b + 1) * BLOCK, :]
                    weight = jnp.exp2(part * log_scale - shift)
                    total = total + jnp.sum(weight, axis=0, keepdims=True)
                    low.append(weight.astype(BF16))
                low = jnp.concatenate(low, axis=0)
                weights[group, :, cols] = low
                group_max[group, :, cols] = peak
                old = run_max[:, cols]
                new = jnp.maximum(old, peak)
                keep, add = jnp.exp2(old - new), jnp.exp2(peak - new)
                run_max[:, cols] = new
                run_total[:, cols] = run_total[:, cols] * keep + total * add
                out_acc[:, cols] = out_acc[:, cols] * keep + dot_nn(values_turned, low) * add
                peaks = later

        forward_heads(0, heads // 2)

        @pl.when(more)
        def _():
            stage_x(k + 1)

        forward_heads(heads // 2, heads)

        @pl.when(more)
        def _():
            stage_core(k + 1)

        return 0

    lax.fori_loop(0, groups, forward_group, 0)

    def stat_copy(head, s):
        return remote(
            stat_recv.at[panel, head], stat_recv.at[panel, head],
            stat_send_sem.at[head, s], stat_recv_sem.at[panel, head],
            {"ka": ring(panel, s, n_ka)},
        )

    def stat_arrived(head, source):
        remote(
            stat_recv.at[source, head], stat_recv.at[source, head],
            stat_send_sem.at[head, 0], stat_recv_sem.at[source, head],
            {"ka": ring(panel, 1, n_ka)},
        ).wait_recv()

    def part_copy(send, recv, send_sem, recv_sem, head):
        local = lax.rem(head, own_heads)
        return remote(
            send.at[head], recv.at[panel, local], send_sem.at[head], recv_sem.at[panel, local],
            {"ka": head // own_heads},
        )

    def part_arrived(recv, send_sem, recv_sem, source, local):
        remote(
            recv.at[source, local], recv.at[source, local],
            send_sem.at[0], recv_sem.at[source, local], {"ka": ring(panel, 1, n_ka)},
        ).wait_recv()

    def finish_head(i, _):
        head = head_at(i)
        cols = head_columns(head)
        total = run_total[:, cols]
        out = out_acc[:, cols] * (1.0 / total)
        delta = jnp.sum(out * do_turned[:, cols].astype(F32), axis=0, keepdims=True)
        stat_recv[panel, head, 0:1, :] = run_max[:, cols] + jnp.log2(total)
        stat_recv[panel, head, 1:2, :] = delta
        for s in range(1, n_ka):
            stat_copy(head, s).start()

        @pl.when(i < heads - own_heads)
        def _():
            out_send[head] = out.astype(BF16)
            part_copy(out_send, out_recv, out_send_sem, out_recv_sem, head).start()

        @pl.when(i >= heads - own_heads)
        def _():
            out_recv[panel, lax.rem(head, own_heads)] = out.astype(BF16)

        return 0

    lax.fori_loop(0, heads, finish_head, 0)

    def merge_head(i, _):
        head = head_at(i)
        cols = head_columns(head)
        for s in range(1, n_ka):
            stat_arrived(head, ring(panel, s, n_ka))
        lses = [stat_recv[n, head, 0:1, :] for n in range(n_ka)]
        peak = functools.reduce(jnp.maximum, lses)
        lse = peak + jnp.log2(sum(jnp.exp2(one - peak) for one in lses))
        row_lse[:, cols] = lse
        row_delta[:, cols] = sum(
            jnp.exp2(lses[n] - lse) * stat_recv[n, head, 1:2, :] for n in range(n_ka)
        )
        return 0

    lax.fori_loop(0, heads, merge_head, 0)

    def back_group_of(k):
        return ring(z, k + 1, groups)

    def core_sum_copy(k):
        return remote(
            core_send.at[k], core_recv.at[k], core_send_sem.at[k], core_recv_sem.at[k],
            {"pb": core_peer},
        )

    def x_sum_copy(k):
        return remote(
            x_send.at[k], x_recv.at[k], x_send_sem.at[k], x_recv_sem.at[k], {"pb": x_peer}
        )

    def z_sum_copy(k):
        return remote(
            z_send.at[k], z_recv.at[k], z_send_sem.at[k], z_recv_sem.at[k],
            {"pb": at(back_group_of(k), x, core)},
        )

    def send_core(k):
        slot = lax.rem(k, 2)
        for part in range(2):
            core_send[k, part] = acc[slot, 2 * part + other_core].astype(BF16)
        core_sum_copy(k).start()

    def send_x(k):
        slot = lax.rem(k, 2)
        core_sum_copy(k).wait_recv()
        passed = acc[slot, 2 * other_x + core] + core_recv[k, other_x].astype(F32)
        x_send[k] = passed.astype(BF16)
        x_sum_copy(k).start()
        mine = 2 * x + core
        acc[slot, mine] = acc[slot, mine] + core_recv[k, x].astype(F32)

    def x_total(k):
        x_sum_copy(k).wait_recv()
        return acc[lax.rem(k, 2), 2 * x + core] + x_recv[k].astype(F32)

    def send_z(k):
        z_send[k] = x_total(k).astype(BF16)
        z_sum_copy(k).start()

    def backward_group(k, _):
        group = back_group_of(k)
        slot = lax.rem(k, 2)

        def rows_of(i):
            return pl.ds(pl.multiple_of(head_at(i) * rows, rows), rows)

        def backward_heads(first, last):
            def dprob(i):
                return dot_nn(group_rows(group, chunk), do_turned[:, head_columns(head_at(i))])

            dprobs = dprob(first)
            for i in range(first, last):
                later = dprob(i + 1) if i + 1 < last else None
                cols = head_columns(head_at(i))
                mix = jnp.exp2(group_max[group, :, cols] - row_lse[:, cols])
                low = weights[group, :, cols] * mix.astype(BF16)
                place = pl.ds(i * rows, rows)
                probs[:, place] = low
                ds = low * (dprobs - row_delta[:, cols]).astype(BF16)
                dscores[:, place] = ds
                dq_acc[:, cols] = dq_acc[:, cols] + dot_nn(k_turned[group], ds)
                dprobs = later

        def send_dq(first, last):
            for i in range(first, min(last, heads - own_heads)):
                head = head_at(i)
                dq_send[head] = (dq_acc[:, head_columns(head)] * scale).astype(BF16)
                part_copy(dq_send, dq_recv, dq_send_sem, dq_recv_sem, head).start()

        def grads(first, last):
            span = slice(first * rows, last * rows)
            q_part = jnp.concatenate([q_rows[rows_of(i), :] for i in range(first, last)], axis=0)
            do_part = jnp.concatenate([do_rows[rows_of(i), :] for i in range(first, last)], axis=0)
            return dot_nn(dscores[:, span], q_part), dot_nn(probs[:, span], do_part)

        half = heads // 2
        backward_heads(0, half)

        @pl.when(k == groups - 1)
        def _():
            send_dq(0, half)

        @pl.when(k > 0)
        def _():
            send_x(k - 1)

        key_part, value_part = grads(0, half)
        backward_heads(half, heads)
        key_more, value_more = grads(half, heads)

        @pl.when(k == groups - 1)
        def _():
            send_dq(half, heads)

        @pl.when(k > 0)
        def _():
            send_z(k - 1)

        acc[slot, :, 0:chunk, :] = ((key_part + key_more) * scale).reshape(4, chunk, dim)
        acc[slot, :, chunk : 2 * chunk, :] = (value_part + value_more).reshape(4, chunk, dim)
        send_core(k)
        return 0

    lax.fori_loop(0, groups, backward_group, 0)

    for local in range(own_heads):
        head = panel * own_heads + local
        cols = head_columns(head)
        for s in range(1, n_ka):
            part_arrived(out_recv, out_send_sem, out_recv_sem, ring(panel, s, n_ka), local)
        lse = row_lse[:, cols]
        mixed = sum(
            jnp.exp2(stat_recv[n, head, 0:1, :] - lse) * out_recv[n, local].astype(F32)
            for n in range(n_ka)
        )
        att_ref[:, local * dim : (local + 1) * dim] = mixed.T.astype(BF16)
        dq_recv[panel, local] = (dq_acc[:, cols] * scale).astype(BF16)

    last = groups - 1
    send_x(last)
    total = x_total(last)
    for k in range(last):
        z_sum_copy(k).wait_recv()
        total = total + z_recv[k].astype(F32)
    kg_ref[...] = total[0:chunk]
    vg_ref[...] = total[chunk : 2 * chunk]

    for local in range(own_heads):
        for s in range(1, n_ka):
            part_arrived(dq_recv, dq_send_sem, dq_recv_sem, ring(panel, s, n_ka), local)
        summed = sum(dq_recv[n, local].astype(F32) for n in range(n_ka))
        qg_ref[:, local * dim : (local + 1) * dim] = summed.T

    def drain_group(k, _):
        x_copy(k).wait_send()
        core_copy(k, 0).wait_send()
        core_copy(k, 1).wait_send()
        core_sum_copy(k).wait_send()
        x_sum_copy(k).wait_send()

        @pl.when(k < last)
        def _():
            z_copy(k + 1).wait_send()
            z_sum_copy(k).wait_send()

        return 0

    lax.fori_loop(0, groups, drain_group, 0)

    def drain_head(i, _):
        head = head_at(i)
        for s in range(1, n_ka):
            stat_copy(head, s).wait_send()

        @pl.when(i < heads - own_heads)
        def _():
            part_copy(out_send, out_recv, out_send_sem, out_recv_sem, head).wait_send()
            part_copy(dq_send, dq_recv, dq_send_sem, dq_recv_sem, head).wait_send()

        return 0

    lax.fori_loop(0, heads, drain_head, 0)


def hand_over(a, b, c, d, a_out, b_out, c_out, d_out, sem):
    pairs = ((a, a_out), (b, b_out), (c, c_out), (d, d_out))
    copies = [pltpu.make_async_copy(src, dst, sem.at[i]) for i, (src, dst) in enumerate(pairs)]
    for copy in copies:
        copy.start()
    for copy in copies:
        copy.wait()


def per_device(n_pb, n_ka, queries, keys, values, dout, block_mask):
    rows, width = queries.shape
    chunk, dim = keys.shape
    heads = width // dim
    own_heads = heads // n_ka
    groups = n_pb // 4
    group_keys = 4 * chunk
    wide = heads * rows
    assert rows == 2 * BLOCK and group_keys % BLOCK == 0
    vmem, dma = pltpu.VMEM, pltpu.SemaphoreType.DMA
    pair = (2 * chunk, dim)
    results = pl.pallas_call(
        functools.partial(kernel, n_pb, n_ka),
        out_shape=(
            jax.ShapeDtypeStruct((rows, own_heads * dim), BF16),
            jax.ShapeDtypeStruct((rows, own_heads * dim), F32),
            jax.ShapeDtypeStruct((chunk, dim), F32),
            jax.ShapeDtypeStruct((chunk, dim), F32),
        ),
        in_specs=[pl.BlockSpec(memory_space=pltpu.SMEM)]
        + [pl.BlockSpec(memory_space=pl.ANY)] * 4,
        out_specs=[pl.BlockSpec(memory_space=pltpu.VMEM)] * 4,
        scratch_shapes=[
            vmem((n_pb,) + pair, BF16),
            vmem((groups, dim, group_keys), BF16),
            vmem((wide, dim), BF16),
            vmem((wide, dim), BF16),
            vmem((dim, wide), BF16),
            vmem((dim, wide), BF16),
            vmem((groups, group_keys, wide), BF16),
            vmem((heads // 2, group_keys, rows), F32),
            vmem((group_keys, wide), BF16),
            vmem((group_keys, wide), BF16),
            vmem((dim, wide), F32),
            vmem((dim, wide), F32),
            vmem((1, wide), F32),
            vmem((1, wide), F32),
            vmem((groups, 1, wide), F32),
            vmem((1, wide), F32),
            vmem((1, wide), F32),
            vmem((n_ka, heads, 8, rows), F32),
            vmem((heads, dim, rows), BF16),
            vmem((n_ka, own_heads, dim, rows), BF16),
            vmem((heads, dim, rows), BF16),
            vmem((n_ka, own_heads, dim, rows), BF16),
            vmem((2, 4) + pair, F32),
            vmem((groups, 2) + pair, BF16),
            vmem((groups, 2) + pair, BF16),
            vmem((groups,) + pair, BF16),
            vmem((groups,) + pair, BF16),
            vmem((groups,) + pair, BF16),
            vmem((groups,) + pair, BF16),
            dma((2 + 2 * heads,)),
            dma((n_pb,)),
            dma((groups,)),
            dma((groups,)),
            dma((2 * groups,)),
            dma((heads, n_ka)),
            dma((n_ka, heads)),
            dma((heads,)),
            dma((n_ka, own_heads)),
            dma((heads,)),
            dma((n_ka, own_heads)),
            dma((groups,)),
            dma((groups,)),
            dma((groups,)),
            dma((groups,)),
            dma((groups,)),
            dma((groups,)),
        ],
        compiler_params=pltpu.CompilerParams(
            collective_id=0, has_side_effects=True, vmem_limit_bytes=58 * 2**20
        ),
        cost_estimate=pl.CostEstimate(
            flops=12 * wide * n_pb * chunk * dim,
            bytes_accessed=4 * rows * width * 2,
            transcendentals=wide * n_pb * chunk,
        ),
    )(block_mask, queries, keys, values, dout)
    return pl.pallas_call(
        hand_over,
        out_shape=tuple(jax.ShapeDtypeStruct(one.shape, one.dtype) for one in results),
        in_specs=[pl.BlockSpec(memory_space=pl.ANY)] * 4,
        out_specs=[pl.BlockSpec(memory_space=pl.ANY)] * 4,
        scratch_shapes=[dma((4,))],
        compiler_params=pltpu.CompilerParams(vmem_limit_bytes=63 * 2**20),
    )(*results)


def solution(mesh):
    in_specs = (
        P("pb", None),
        P(("ka", "pb"), None),
        P(("ka", "pb"), None),
        P("pb", None),
        P("pb", "ka"),
    )
    out_specs = (P("pb", "ka"), P("pb", "ka"), P(("ka", "pb"), None), P(("ka", "pb"), None))
    return jax.shard_map(
        functools.partial(per_device, mesh.shape["pb"], mesh.shape["ka"]),
        mesh=mesh, in_specs=in_specs, out_specs=out_specs, check_vma=False,
    )
```

```python
import functools
import math

import jax
import jax.numpy as jnp
from jax import lax
from jax.experimental import pallas as pl
from jax.experimental.pallas import tpu as pltpu
from jax.sharding import PartitionSpec as P

BLOCK = 128
DEAD = 1e30
F32 = jnp.float32
BF16 = jnp.bfloat16


def dot_nn(a, b):
    return jnp.dot(a, b, preferred_element_type=F32)


def dot_nt(a, b):
    return lax.dot_general(a, b, (((1,), (1,)), ((), ())), preferred_element_type=F32)


def kernel(
    n_pb, n_ka,
    mask_ref, q_ref, k_ref, v_ref, do_ref,
    att_ref, qg_ref, kg_ref, vg_ref,
    kv, k_turned, q_rows, do_rows, q_turned, do_turned, weights, wide_scores, probs, dscores,
    out_acc, dq_acc, run_max, run_total, group_max, row_lse, row_delta,
    stat_recv, out_send, out_recv, dq_send, dq_recv,
    acc, core_send, core_recv, x_send, x_recv, z_send, z_recv,
    load_sem, ag_recv_sem, ag_z_sem, ag_x_sem, ag_core_sem,
    stat_send_sem, stat_recv_sem, out_send_sem, out_recv_sem, dq_send_sem, dq_recv_sem,
    core_send_sem, core_recv_sem, x_send_sem, x_recv_sem, z_send_sem, z_recv_sem,
):
    rows, width = q_ref.shape
    chunk, dim = k_ref.shape
    heads = width // dim
    own_heads = heads // n_ka
    groups = n_pb // 4
    group_keys = 4 * chunk
    group_blocks = group_keys // BLOCK
    scale = 1.0 / math.sqrt(dim)
    log_scale = scale * math.log2(math.e)

    me = lax.axis_index("pb")
    panel = lax.axis_index("ka")
    core = lax.rem(me, 2)
    x = lax.rem(me // 2, 2)
    z = me // 4
    other_core, other_x = 1 - core, 1 - x

    def at(z_index, x_index, core_index):
        return (z_index * 2 + x_index) * 2 + core_index

    core_peer, x_peer = at(z, x, other_core), at(z, other_x, core)

    def remote(src, dst, send_sem, recv_sem, device):
        return pltpu.make_async_remote_copy(
            src_ref=src, dst_ref=dst, send_sem=send_sem, recv_sem=recv_sem,
            device_id=device, device_id_type=pl.DeviceIdType.MESH,
        )

    def ring(start, step, size):
        return lax.rem(start + step, size)

    def load(index, src, dst):
        return pltpu.make_async_copy(src, dst, load_sem.at[index])

    loads = [
        load(0, k_ref, kv.at[me, pl.ds(0, chunk)]),
        load(1, v_ref, kv.at[me, pl.ds(chunk, chunk)]),
    ]
    for part, (src, dst) in enumerate(((q_ref, q_rows), (do_ref, do_rows))):
        for head in range(heads):
            loads.append(
                load(
                    2 + part * heads + head,
                    src.at[:, pl.ds(head * dim, dim)],
                    dst.at[pl.ds(head * rows, rows), :],
                )
            )
    for one in loads:
        one.start()

    barrier = pltpu.get_barrier_semaphore()
    partners = [{"pb": core_peer}, {"pb": x_peer}]
    partners += [{"pb": at(ring(z, s, groups), x, core)} for s in range(1, groups)]
    partners += [{"ka": ring(panel, s, n_ka)} for s in range(1, n_ka)]
    for partner in partners:
        pl.semaphore_signal(barrier, inc=1, device_id=partner, device_id_type=pl.DeviceIdType.MESH)
    loads[0].wait()
    loads[1].wait()
    pl.semaphore_wait(barrier, len(partners))

    def gather_copy(index, send_sem, device):
        return remote(kv.at[index], kv.at[index], send_sem, ag_recv_sem.at[index], {"pb": device})

    def z_copy(s):
        return gather_copy(me, ag_z_sem.at[s], at(ring(z, s, groups), x, core))

    def x_copy(k):
        return gather_copy(at(ring(z, k, groups), x, core), ag_x_sem.at[k], x_peer)

    def core_copy(k, part):
        owner_x = x if part == 0 else other_x
        index = at(ring(z, k, groups), owner_x, core)
        return gather_copy(index, ag_core_sem.at[2 * k + part], core_peer)

    def arrived(index):
        gather_copy(index, ag_x_sem.at[0], core_peer).wait_recv()

    x_copy(0).start()
    core_copy(0, 0).start()
    for s in range(1, groups):
        z_copy(s).start()

    def head_columns(head, count=1):
        return pl.ds(pl.multiple_of(head * rows, rows), count * rows)

    def head_at(i):
        return lax.rem((panel + 1) * own_heads + i, heads) if own_heads % 2 == 0 else i

    def foreign(head):
        return head // own_heads != panel

    for one in loads[2:]:
        one.wait()
    for head in range(heads):
        span = pl.ds(head * rows, rows)
        q_turned[:, span] = q_rows[span, :].T
        do_turned[:, span] = do_rows[span, :].T
    out_acc[...] = jnp.zeros_like(out_acc)
    dq_acc[...] = jnp.zeros_like(dq_acc)
    run_max[...] = jnp.full_like(run_max, -1e38)
    run_total[...] = jnp.zeros_like(run_total)

    def stage_x(k):
        arrived(at(ring(z, k, groups), other_x, core))
        core_copy(k, 1).start()

    def stage_core(k):
        arrived(at(ring(z, k, groups), x, other_core))
        arrived(at(ring(z, k, groups), other_x, other_core))

    stage_x(0)
    stage_core(0)

    def group_rows(group, first):
        return kv[pl.ds(group * 4, 4), first : first + chunk, :].reshape(group_keys, dim)

    def forward_group(k, _):
        group = ring(z, k, groups)
        more = k < groups - 1

        @pl.when(more)
        def _():
            arrived(at(ring(z, k + 1, groups), x, core))
            x_copy(k + 1).start()
            core_copy(k + 1, 0).start()

        keys = group_rows(group, 0)
        k_turned[group] = keys.T
        values_turned = group_rows(group, chunk).T
        bias = [
            (mask_ref[0, group * group_blocks + b].astype(F32) - 1.0) * DEAD
            for b in range(group_blocks)
        ]

        def forward_heads(first, last):
            def score(i):
                scores = dot_nn(group_rows(group, 0), q_turned[:, head_columns(head_at(i), 2)])
                wide_scores[(i - first) // 2] = scores
                return [
                    jnp.max(scores[b * BLOCK : (b + 1) * BLOCK], axis=0, keepdims=True) * log_scale
                    for b in range(group_blocks)
                ]

            peaks = score(first)
            for i in range(first, last, 2):
                later = score(i + 2) if i + 2 < last else None
                cols = head_columns(head_at(i), 2)
                peak = functools.reduce(jnp.maximum, [p + one for p, one in zip(peaks, bias)])
                low = []
                total = jnp.zeros_like(peak)
                for b in range(group_blocks):
                    shift = jnp.maximum(peak - bias[b], peaks[b])
                    part = wide_scores[(i - first) // 2, b * BLOCK : (b + 1) * BLOCK, :]
                    weight = jnp.exp2(part * log_scale - shift)
                    total = total + jnp.sum(weight, axis=0, keepdims=True)
                    low.append(weight.astype(BF16))
                low = jnp.concatenate(low, axis=0)
                weights[group, :, cols] = low
                group_max[group, :, cols] = peak
                old = run_max[:, cols]
                new = jnp.maximum(old, peak)
                keep, add = jnp.exp2(old - new), jnp.exp2(peak - new)
                run_max[:, cols] = new
                run_total[:, cols] = run_total[:, cols] * keep + total * add
                out_acc[:, cols] = out_acc[:, cols] * keep + dot_nn(values_turned, low) * add
                peaks = later

        forward_heads(0, heads // 2)

        @pl.when(more)
        def _():
            stage_x(k + 1)

        forward_heads(heads // 2, heads)

        @pl.when(more)
        def _():
            stage_core(k + 1)

        return 0

    lax.fori_loop(0, groups, forward_group, 0)

    def stat_copy(head, s):
        return remote(
            stat_recv.at[panel, head], stat_recv.at[panel, head],
            stat_send_sem.at[head, s], stat_recv_sem.at[panel, head],
            {"ka": ring(panel, s, n_ka)},
        )

    def stat_arrived(head, source):
        remote(
            stat_recv.at[source, head], stat_recv.at[source, head],
            stat_send_sem.at[head, 0], stat_recv_sem.at[source, head],
            {"ka": ring(panel, 1, n_ka)},
        ).wait_recv()

    def part_copy(send, recv, send_sem, recv_sem, head):
        local = lax.rem(head, own_heads)
        return remote(
            send.at[head], recv.at[panel, local], send_sem.at[head], recv_sem.at[panel, local],
            {"ka": head // own_heads},
        )

    def part_arrived(recv, send_sem, recv_sem, source, local):
        remote(
            recv.at[source, local], recv.at[source, local],
            send_sem.at[0], recv_sem.at[source, local], {"ka": ring(panel, 1, n_ka)},
        ).wait_recv()

    def finish_head(i, _):
        head = head_at(i)
        cols = head_columns(head)
        total = run_total[:, cols]
        out = out_acc[:, cols] * (1.0 / total)
        delta = jnp.sum(out * do_turned[:, cols].astype(F32), axis=0, keepdims=True)
        stat_recv[panel, head, 0:1, :] = run_max[:, cols] + jnp.log2(total)
        stat_recv[panel, head, 1:2, :] = delta
        for s in range(1, n_ka):
            stat_copy(head, s).start()

        @pl.when(foreign(head))
        def _():
            out_send[head] = out.astype(BF16)
            part_copy(out_send, out_recv, out_send_sem, out_recv_sem, head).start()

        @pl.when(jnp.logical_not(foreign(head)))
        def _():
            out_recv[panel, lax.rem(head, own_heads)] = out.astype(BF16)

        return 0

    lax.fori_loop(0, heads, finish_head, 0)

    def merge_head(i, _):
        head = head_at(i)
        cols = head_columns(head)
        for s in range(1, n_ka):
            stat_arrived(head, ring(panel, s, n_ka))
        lses = [stat_recv[n, head, 0:1, :] for n in range(n_ka)]
        peak = functools.reduce(jnp.maximum, lses)
        lse = peak + jnp.log2(sum(jnp.exp2(one - peak) for one in lses))
        row_lse[:, cols] = lse
        row_delta[:, cols] = sum(
            jnp.exp2(lses[n] - lse) * stat_recv[n, head, 1:2, :] for n in range(n_ka)
        )
        return 0

    lax.fori_loop(0, heads, merge_head, 0)

    def back_group_of(k):
        return ring(z, k + 1, groups)

    def core_sum_copy(k):
        return remote(
            core_send.at[k], core_recv.at[k], core_send_sem.at[k], core_recv_sem.at[k],
            {"pb": core_peer},
        )

    def x_sum_copy(k):
        return remote(
            x_send.at[k], x_recv.at[k], x_send_sem.at[k], x_recv_sem.at[k], {"pb": x_peer}
        )

    def z_sum_copy(k):
        return remote(
            z_send.at[k], z_recv.at[k], z_send_sem.at[k], z_recv_sem.at[k],
            {"pb": at(back_group_of(k), x, core)},
        )

    def send_core(k):
        slot = lax.rem(k, 2)
        for part in range(2):
            core_send[k, part] = acc[slot, 2 * part + other_core].astype(BF16)
        core_sum_copy(k).start()

    def send_x(k):
        slot = lax.rem(k, 2)
        core_sum_copy(k).wait_recv()
        passed = acc[slot, 2 * other_x + core] + core_recv[k, other_x].astype(F32)
        x_send[k] = passed.astype(BF16)
        x_sum_copy(k).start()
        mine = 2 * x + core
        acc[slot, mine] = acc[slot, mine] + core_recv[k, x].astype(F32)

    def x_total(k):
        x_sum_copy(k).wait_recv()
        return acc[lax.rem(k, 2), 2 * x + core] + x_recv[k].astype(F32)

    def send_z(k):
        z_send[k] = x_total(k).astype(BF16)
        z_sum_copy(k).start()

    def backward_group(k, _):
        group = back_group_of(k)
        slot = lax.rem(k, 2)

        def rows_of(i):
            return pl.ds(pl.multiple_of(head_at(i) * rows, rows), rows)

        def backward_heads(first, last):
            def add_dq(i):
                cols = head_columns(head_at(i), 2)
                ds = dscores[:, i * rows : (i + 2) * rows]
                dq_acc[:, cols] = dq_acc[:, cols] + dot_nn(k_turned[group], ds)

            for i in range(first, last, 2):
                cols = head_columns(head_at(i), 2)
                place = slice(i * rows, (i + 2) * rows)
                mix = jnp.exp2(group_max[group, :, cols] - row_lse[:, cols])
                dprobs = dot_nn(group_rows(group, chunk), do_turned[:, cols])
                low = weights[group, :, cols] * mix.astype(BF16)
                probs[:, place] = low
                dscores[:, place] = low * (dprobs - row_delta[:, cols]).astype(BF16)
                if i > first:
                    add_dq(i - 2)
            add_dq(last - 2)

        def send_dq(first, last):
            def send(i, _):
                head = head_at(i)

                @pl.when(foreign(head))
                def _():
                    dq_send[head] = (dq_acc[:, head_columns(head)] * scale).astype(BF16)
                    part_copy(dq_send, dq_recv, dq_send_sem, dq_recv_sem, head).start()

                return 0

            lax.fori_loop(first, last, send, 0)

        def grads(first, last):
            span = slice(first * rows, last * rows)
            q_part = jnp.concatenate([q_rows[rows_of(i), :] for i in range(first, last)], axis=0)
            do_part = jnp.concatenate([do_rows[rows_of(i), :] for i in range(first, last)], axis=0)
            return dot_nn(dscores[:, span], q_part), dot_nn(probs[:, span], do_part)

        half = heads // 2
        backward_heads(0, half)

        @pl.when(k == groups - 1)
        def _():
            send_dq(0, half)

        @pl.when(k > 0)
        def _():
            send_x(k - 1)

        key_part, value_part = grads(0, half)
        backward_heads(half, heads)
        key_more, value_more = grads(half, heads)

        @pl.when(k == groups - 1)
        def _():
            send_dq(half, heads)

        @pl.when(k > 0)
        def _():
            send_z(k - 1)

        acc[slot, :, 0:chunk, :] = ((key_part + key_more) * scale).reshape(4, chunk, dim)
        acc[slot, :, chunk : 2 * chunk, :] = (value_part + value_more).reshape(4, chunk, dim)
        send_core(k)
        return 0

    lax.fori_loop(0, groups, backward_group, 0)

    for local in range(own_heads):
        head = panel * own_heads + local
        cols = head_columns(head)
        for s in range(1, n_ka):
            part_arrived(out_recv, out_send_sem, out_recv_sem, ring(panel, s, n_ka), local)
        lse = row_lse[:, cols]
        mixed = sum(
            jnp.exp2(stat_recv[n, head, 0:1, :] - lse) * out_recv[n, local].astype(F32)
            for n in range(n_ka)
        )
        att_ref[:, local * dim : (local + 1) * dim] = mixed.T.astype(BF16)
        dq_recv[panel, local] = (dq_acc[:, cols] * scale).astype(BF16)

    last = groups - 1
    send_x(last)
    total = x_total(last)
    for k in range(last):
        z_sum_copy(k).wait_recv()
        total = total + z_recv[k].astype(F32)
    kg_ref[...] = total[0:chunk]
    vg_ref[...] = total[chunk : 2 * chunk]

    for local in range(own_heads):
        for s in range(1, n_ka):
            part_arrived(dq_recv, dq_send_sem, dq_recv_sem, ring(panel, s, n_ka), local)
        summed = sum(dq_recv[n, local].astype(F32) for n in range(n_ka))
        qg_ref[:, local * dim : (local + 1) * dim] = summed.T

    def drain_group(k, _):
        x_copy(k).wait_send()
        core_copy(k, 0).wait_send()
        core_copy(k, 1).wait_send()
        core_sum_copy(k).wait_send()
        x_sum_copy(k).wait_send()

        @pl.when(k < last)
        def _():
            z_copy(k + 1).wait_send()
            z_sum_copy(k).wait_send()

        return 0

    lax.fori_loop(0, groups, drain_group, 0)

    def drain_head(i, _):
        head = head_at(i)
        for s in range(1, n_ka):
            stat_copy(head, s).wait_send()

        @pl.when(foreign(head))
        def _():
            part_copy(out_send, out_recv, out_send_sem, out_recv_sem, head).wait_send()
            part_copy(dq_send, dq_recv, dq_send_sem, dq_recv_sem, head).wait_send()

        return 0

    lax.fori_loop(0, heads, drain_head, 0)


def hand_over(a, b, c, d, a_out, b_out, c_out, d_out, sem):
    pairs = ((a, a_out), (b, b_out), (c, c_out), (d, d_out))
    copies = [pltpu.make_async_copy(src, dst, sem.at[i]) for i, (src, dst) in enumerate(pairs)]
    for copy in copies:
        copy.start()
    for copy in copies:
        copy.wait()


def per_device(n_pb, n_ka, queries, keys, values, dout, block_mask):
    rows, width = queries.shape
    chunk, dim = keys.shape
    heads = width // dim
    own_heads = heads // n_ka
    groups = n_pb // 4
    group_keys = 4 * chunk
    wide = heads * rows
    assert rows == 2 * BLOCK and heads % 4 == 0 and group_keys % BLOCK == 0
    vmem, dma = pltpu.VMEM, pltpu.SemaphoreType.DMA
    pair = (2 * chunk, dim)
    results = pl.pallas_call(
        functools.partial(kernel, n_pb, n_ka),
        out_shape=(
            jax.ShapeDtypeStruct((rows, own_heads * dim), BF16),
            jax.ShapeDtypeStruct((rows, own_heads * dim), F32),
            jax.ShapeDtypeStruct((chunk, dim), F32),
            jax.ShapeDtypeStruct((chunk, dim), F32),
        ),
        in_specs=[pl.BlockSpec(memory_space=pltpu.SMEM)]
        + [pl.BlockSpec(memory_space=pl.ANY)] * 4,
        out_specs=[pl.BlockSpec(memory_space=pltpu.VMEM)] * 4,
        scratch_shapes=[
            vmem((n_pb,) + pair, BF16),
            vmem((groups, dim, group_keys), BF16),
            vmem((wide, dim), BF16),
            vmem((wide, dim), BF16),
            vmem((dim, wide), BF16),
            vmem((dim, wide), BF16),
            vmem((groups, group_keys, wide), BF16),
            vmem((heads // 4, group_keys, 2 * rows), F32),
            vmem((group_keys, wide), BF16),
            vmem((group_keys, wide), BF16),
            vmem((dim, wide), F32),
            vmem((dim, wide), F32),
            vmem((1, wide), F32),
            vmem((1, wide), F32),
            vmem((groups, 1, wide), F32),
            vmem((1, wide), F32),
            vmem((1, wide), F32),
            vmem((n_ka, heads, 8, rows), F32),
            vmem((heads, dim, rows), BF16),
            vmem((n_ka, own_heads, dim, rows), BF16),
            vmem((heads, dim, rows), BF16),
            vmem((n_ka, own_heads, dim, rows), BF16),
            vmem((2, 4) + pair, F32),
            vmem((groups, 2) + pair, BF16),
            vmem((groups, 2) + pair, BF16),
            vmem((groups,) + pair, BF16),
            vmem((groups,) + pair, BF16),
            vmem((groups,) + pair, BF16),
            vmem((groups,) + pair, BF16),
            dma((2 + 2 * heads,)),
            dma((n_pb,)),
            dma((groups,)),
            dma((groups,)),
            dma((2 * groups,)),
            dma((heads, n_ka)),
            dma((n_ka, heads)),
            dma((heads,)),
            dma((n_ka, own_heads)),
            dma((heads,)),
            dma((n_ka, own_heads)),
            dma((groups,)),
            dma((groups,)),
            dma((groups,)),
            dma((groups,)),
            dma((groups,)),
            dma((groups,)),
        ],
        compiler_params=pltpu.CompilerParams(
            collective_id=0, has_side_effects=True, vmem_limit_bytes=58 * 2**20
        ),
        cost_estimate=pl.CostEstimate(
            flops=12 * wide * n_pb * chunk * dim,
            bytes_accessed=4 * rows * width * 2,
            transcendentals=wide * n_pb * chunk,
        ),
    )(block_mask, queries, keys, values, dout)
    return pl.pallas_call(
        hand_over,
        out_shape=tuple(jax.ShapeDtypeStruct(one.shape, one.dtype) for one in results),
        in_specs=[pl.BlockSpec(memory_space=pl.ANY)] * 4,
        out_specs=[pl.BlockSpec(memory_space=pltpu.VMEM)] * 4,
        scratch_shapes=[dma((4,))],
        compiler_params=pltpu.CompilerParams(vmem_limit_bytes=63 * 2**20),
    )(*results)


def solution(mesh):
    in_specs = (
        P("pb", None),
        P(("ka", "pb"), None),
        P(("ka", "pb"), None),
        P("pb", None),
        P("pb", "ka"),
    )
    out_specs = (P("pb", "ka"), P("pb", "ka"), P(("ka", "pb"), None), P(("ka", "pb"), None))
    return jax.shard_map(
        functools.partial(per_device, mesh.shape["pb"], mesh.shape["ka"]),
        mesh=mesh, in_specs=in_specs, out_specs=out_specs, check_vma=False,
    )
```

```python
import functools
import math

import jax
import jax.numpy as jnp
from jax import lax
from jax.experimental import pallas as pl
from jax.experimental.pallas import tpu as pltpu
from jax.sharding import PartitionSpec as P

BLOCK = 128
DEAD = 1e30
F32 = jnp.float32
BF16 = jnp.bfloat16


def dot_nn(a, b):
    return jnp.dot(a, b, preferred_element_type=F32)


def dot_nt(a, b):
    return lax.dot_general(a, b, (((1,), (1,)), ((), ())), preferred_element_type=F32)


def kernel(
    n_pb, n_ka,
    mask_ref, q_ref, k_ref, v_ref, do_ref,
    att_ref, qg_ref, kg_ref, vg_ref,
    kv, k_turned, q_rows, do_rows, q_turned, do_turned, weights, wide_scores, probs, dscores,
    out_acc, dq_acc, run_max, run_total, group_max, row_lse, row_delta,
    stat_recv, out_send, out_recv, dq_send, dq_recv,
    acc, core_send, core_recv, x_send, x_recv, z_send, z_recv,
    load_sem, ag_recv_sem, ag_z_sem, ag_x_sem, ag_core_sem,
    stat_send_sem, stat_recv_sem, out_send_sem, out_recv_sem, dq_send_sem, dq_recv_sem,
    core_send_sem, core_recv_sem, x_send_sem, x_recv_sem, z_send_sem, z_recv_sem,
):
    rows, width = q_ref.shape
    chunk, dim = k_ref.shape
    heads = width // dim
    own_heads = heads // n_ka
    groups = n_pb // 4
    group_keys = 4 * chunk
    group_blocks = group_keys // BLOCK
    scale = 1.0 / math.sqrt(dim)
    log_scale = scale * math.log2(math.e)

    me = lax.axis_index("pb")
    panel = lax.axis_index("ka")
    core = lax.rem(me, 2)
    x = lax.rem(me // 2, 2)
    z = me // 4
    other_core, other_x = 1 - core, 1 - x

    def at(z_index, x_index, core_index):
        return (z_index * 2 + x_index) * 2 + core_index

    core_peer, x_peer = at(z, x, other_core), at(z, other_x, core)

    def remote(src, dst, send_sem, recv_sem, device):
        return pltpu.make_async_remote_copy(
            src_ref=src, dst_ref=dst, send_sem=send_sem, recv_sem=recv_sem,
            device_id=device, device_id_type=pl.DeviceIdType.MESH,
        )

    def ring(start, step, size):
        return lax.rem(start + step, size)

    def load(index, src, dst):
        return pltpu.make_async_copy(src, dst, load_sem.at[index])

    loads = [
        load(0, k_ref, kv.at[me, pl.ds(0, chunk)]),
        load(1, v_ref, kv.at[me, pl.ds(chunk, chunk)]),
    ]
    for part, (src, dst) in enumerate(((q_ref, q_rows), (do_ref, do_rows))):
        for head in range(heads):
            loads.append(
                load(
                    2 + part * heads + head,
                    src.at[:, pl.ds(head * dim, dim)],
                    dst.at[pl.ds(head * rows, rows), :],
                )
            )
    for one in loads:
        one.start()

    barrier = pltpu.get_barrier_semaphore()
    partners = [{"pb": core_peer}, {"pb": x_peer}]
    partners += [{"pb": at(ring(z, s, groups), x, core)} for s in range(1, groups)]
    partners += [{"ka": ring(panel, s, n_ka)} for s in range(1, n_ka)]
    for partner in partners:
        pl.semaphore_signal(barrier, inc=1, device_id=partner, device_id_type=pl.DeviceIdType.MESH)
    loads[0].wait()
    loads[1].wait()
    pl.semaphore_wait(barrier, len(partners))

    def gather_copy(index, send_sem, device):
        return remote(kv.at[index], kv.at[index], send_sem, ag_recv_sem.at[index], {"pb": device})

    def z_copy(s):
        return gather_copy(me, ag_z_sem.at[s], at(ring(z, s, groups), x, core))

    def x_copy(k):
        return gather_copy(at(ring(z, k, groups), x, core), ag_x_sem.at[k], x_peer)

    def core_copy(k, part):
        owner_x = x if part == 0 else other_x
        index = at(ring(z, k, groups), owner_x, core)
        return gather_copy(index, ag_core_sem.at[2 * k + part], core_peer)

    def arrived(index):
        gather_copy(index, ag_x_sem.at[0], core_peer).wait_recv()

    x_copy(0).start()
    core_copy(0, 0).start()
    for s in range(1, groups):
        z_copy(s).start()

    def head_columns(head, count=1):
        return pl.ds(pl.multiple_of(head * rows, rows), count * rows)

    def head_at(i):
        return lax.rem((panel + 1) * own_heads + i, heads) if own_heads % 2 == 0 else i

    def foreign(head):
        return head // own_heads != panel

    out_acc[...] = jnp.zeros_like(out_acc)
    dq_acc[...] = jnp.zeros_like(dq_acc)
    run_max[...] = jnp.full_like(run_max, -1e38)
    run_total[...] = jnp.zeros_like(run_total)

    def stage_x(k):
        arrived(at(ring(z, k, groups), other_x, core))
        core_copy(k, 1).start()

    def stage_core(k):
        arrived(at(ring(z, k, groups), x, other_core))
        arrived(at(ring(z, k, groups), other_x, other_core))

    def turn(src, dst, first):
        for head in range(heads):
            loads[first + head].wait()
            span = pl.ds(head * rows, rows)
            dst[:, span] = src[span, :].T

    turn(q_rows, q_turned, 2)
    stage_x(0)
    turn(do_rows, do_turned, 2 + heads)
    stage_core(0)

    def group_rows(group, first):
        return kv[pl.ds(group * 4, 4), first : first + chunk, :].reshape(group_keys, dim)

    def forward_group(k, _):
        group = ring(z, k, groups)
        more = k < groups - 1

        @pl.when(more)
        def _():
            arrived(at(ring(z, k + 1, groups), x, core))
            x_copy(k + 1).start()
            core_copy(k + 1, 0).start()

        keys = group_rows(group, 0)
        k_turned[group] = keys.T
        values_turned = group_rows(group, chunk).T
        bias = [
            (mask_ref[0, group * group_blocks + b].astype(F32) - 1.0) * DEAD
            for b in range(group_blocks)
        ]

        def forward_heads(first, last):
            def score(i):
                scores = dot_nn(group_rows(group, 0), q_turned[:, head_columns(head_at(i), 2)])
                wide_scores[(i - first) // 2] = scores
                return [
                    jnp.max(scores[b * BLOCK : (b + 1) * BLOCK], axis=0, keepdims=True) * log_scale
                    for b in range(group_blocks)
                ]

            peaks = score(first)
            for i in range(first, last, 2):
                later = score(i + 2) if i + 2 < last else None
                cols = head_columns(head_at(i), 2)
                peak = functools.reduce(jnp.maximum, [p + one for p, one in zip(peaks, bias)])
                low = []
                total = jnp.zeros_like(peak)
                for b in range(group_blocks):
                    shift = jnp.maximum(peak - bias[b], peaks[b])
                    part = wide_scores[(i - first) // 2, b * BLOCK : (b + 1) * BLOCK, :]
                    weight = jnp.exp2(part * log_scale - shift)
                    total = total + jnp.sum(weight, axis=0, keepdims=True)
                    low.append(weight.astype(BF16))
                low = jnp.concatenate(low, axis=0)
                weights[group, :, cols] = low
                group_max[group, :, cols] = peak
                old = run_max[:, cols]
                new = jnp.maximum(old, peak)
                keep, add = jnp.exp2(old - new), jnp.exp2(peak - new)
                run_max[:, cols] = new
                run_total[:, cols] = run_total[:, cols] * keep + total * add
                out_acc[:, cols] = out_acc[:, cols] * keep + dot_nn(values_turned, low) * add
                peaks = later

        forward_heads(0, heads // 2)

        @pl.when(more)
        def _():
            stage_x(k + 1)

        forward_heads(heads // 2, heads)

        @pl.when(more)
        def _():
            stage_core(k + 1)

        return 0

    lax.fori_loop(0, groups, forward_group, 0)

    def stat_copy(head, s):
        return remote(
            stat_recv.at[panel, head], stat_recv.at[panel, head],
            stat_send_sem.at[head, s], stat_recv_sem.at[panel, head],
            {"ka": ring(panel, s, n_ka)},
        )

    def stat_arrived(head, source):
        remote(
            stat_recv.at[source, head], stat_recv.at[source, head],
            stat_send_sem.at[head, 0], stat_recv_sem.at[source, head],
            {"ka": ring(panel, 1, n_ka)},
        ).wait_recv()

    def part_copy(send, recv, send_sem, recv_sem, head):
        local = lax.rem(head, own_heads)
        return remote(
            send.at[head], recv.at[panel, local], send_sem.at[head], recv_sem.at[panel, local],
            {"ka": head // own_heads},
        )

    def part_arrived(recv, send_sem, recv_sem, source, local):
        remote(
            recv.at[source, local], recv.at[source, local],
            send_sem.at[0], recv_sem.at[source, local], {"ka": ring(panel, 1, n_ka)},
        ).wait_recv()

    def finish_stats(i, _):
        head = head_at(i)
        cols = head_columns(head)
        total = run_total[:, cols]
        delta = jnp.sum(out_acc[:, cols] * do_turned[:, cols].astype(F32), axis=0, keepdims=True)
        stat_recv[panel, head, 0:1, :] = run_max[:, cols] + jnp.log2(total)
        stat_recv[panel, head, 1:2, :] = delta / total
        for s in range(1, n_ka):
            stat_copy(head, s).start()
        return 0

    def finish_out(i, _):
        head = head_at(i)
        cols = head_columns(head)
        out = (out_acc[:, cols] * (1.0 / run_total[:, cols])).astype(BF16)

        @pl.when(foreign(head))
        def _():
            out_send[head] = out
            part_copy(out_send, out_recv, out_send_sem, out_recv_sem, head).start()

        @pl.when(jnp.logical_not(foreign(head)))
        def _():
            out_recv[panel, lax.rem(head, own_heads)] = out

        return 0

    lax.fori_loop(0, heads, finish_stats, 0)
    lax.fori_loop(0, heads, finish_out, 0)

    def merge_head(i, _):
        head = head_at(i)
        cols = head_columns(head)
        for s in range(1, n_ka):
            stat_arrived(head, ring(panel, s, n_ka))
        lses = [stat_recv[n, head, 0:1, :] for n in range(n_ka)]
        peak = functools.reduce(jnp.maximum, lses)
        lse = peak + jnp.log2(sum(jnp.exp2(one - peak) for one in lses))
        row_lse[:, cols] = lse
        row_delta[:, cols] = sum(
            jnp.exp2(lses[n] - lse) * stat_recv[n, head, 1:2, :] for n in range(n_ka)
        )
        return 0

    half = heads // 2
    lax.fori_loop(0, half, merge_head, 0)

    def back_group_of(k):
        return ring(z, k + 1, groups)

    def core_sum_copy(k):
        return remote(
            core_send.at[k], core_recv.at[k], core_send_sem.at[k], core_recv_sem.at[k],
            {"pb": core_peer},
        )

    def x_sum_copy(k):
        return remote(
            x_send.at[k], x_recv.at[k], x_send_sem.at[k], x_recv_sem.at[k], {"pb": x_peer}
        )

    def z_sum_copy(k):
        return remote(
            z_send.at[k], z_recv.at[k], z_send_sem.at[k], z_recv_sem.at[k],
            {"pb": at(back_group_of(k), x, core)},
        )

    def send_core(k):
        for part in range(2):
            core_send[k, part] = acc[k, 2 * part + other_core].astype(BF16)
        core_sum_copy(k).start()

    def send_x(k):
        core_sum_copy(k).wait_recv()
        passed = acc[k, 2 * other_x + core] + core_recv[k, other_x].astype(F32)
        x_send[k] = passed.astype(BF16)
        x_sum_copy(k).start()
        mine = 2 * x + core
        acc[k, mine] = acc[k, mine] + core_recv[k, x].astype(F32)

    def x_total(k):
        x_sum_copy(k).wait_recv()
        return acc[k, 2 * x + core] + x_recv[k].astype(F32)

    def send_z(k):
        z_send[k] = x_total(k).astype(BF16)
        z_sum_copy(k).start()

    def backward_block(k, first, last):
        group = back_group_of(k)

        def rows_of(i):
            return pl.ds(pl.multiple_of(head_at(i) * rows, rows), rows)

        def backward_heads(first, last):
            def add_dq(i):
                cols = head_columns(head_at(i), 2)
                ds = dscores[:, i * rows : (i + 2) * rows]
                dq_acc[:, cols] = dq_acc[:, cols] + dot_nn(k_turned[group], ds)

            for i in range(first, last, 2):
                cols = head_columns(head_at(i), 2)
                place = slice(i * rows, (i + 2) * rows)
                mix = jnp.exp2(group_max[group, :, cols] - row_lse[:, cols])
                dprobs = dot_nn(group_rows(group, chunk), do_turned[:, cols])
                low = weights[group, :, cols] * mix.astype(BF16)
                probs[:, place] = low
                dscores[:, place] = low * (dprobs - row_delta[:, cols]).astype(BF16)
                if i > first:
                    add_dq(i - 2)
            add_dq(last - 2)

        backward_heads(first, last)
        span = slice(first * rows, last * rows)
        q_part = jnp.concatenate([q_rows[rows_of(i), :] for i in range(first, last)], axis=0)
        do_part = jnp.concatenate([do_rows[rows_of(i), :] for i in range(first, last)], axis=0)
        key_part = dot_nn(dscores[:, span], q_part) * scale
        value_part = dot_nn(probs[:, span], do_part)
        return key_part.reshape(4, chunk, dim), value_part.reshape(4, chunk, dim)

    def send_dq(i, _):
        head = head_at(i)

        @pl.when(foreign(head))
        def _():
            dq_send[head] = (dq_acc[:, head_columns(head)] * scale).astype(BF16)
            part_copy(dq_send, dq_recv, dq_send_sem, dq_recv_sem, head).start()

        return 0

    def sweep_one(k, _):
        key_part, value_part = backward_block(k, 0, half)
        acc[k, :, 0:chunk, :] = key_part
        acc[k, :, chunk : 2 * chunk, :] = value_part
        return 0

    def sweep_two(k, _):
        key_part, value_part = backward_block(k, half, heads)
        acc[k, :, 0:chunk, :] = acc[k, :, 0:chunk, :] + key_part
        acc[k, :, chunk : 2 * chunk, :] = acc[k, :, chunk : 2 * chunk, :] + value_part
        send_core(k)

        @pl.when(k > 0)
        def _():
            send_x(k - 1)

        @pl.when(k > 1)
        def _():
            send_z(k - 2)

        return 0

    lax.fori_loop(0, groups, sweep_one, 0)
    lax.fori_loop(0, half, send_dq, 0)
    lax.fori_loop(half, heads, merge_head, 0)
    lax.fori_loop(0, groups, sweep_two, 0)
    lax.fori_loop(half, heads, send_dq, 0)
    last = groups - 1
    if groups > 1:
        send_z(last - 1)
    send_x(last)

    for local in range(own_heads):
        head = panel * own_heads + local
        cols = head_columns(head)
        for s in range(1, n_ka):
            part_arrived(out_recv, out_send_sem, out_recv_sem, ring(panel, s, n_ka), local)
        lse = row_lse[:, cols]
        mixed = sum(
            jnp.exp2(stat_recv[n, head, 0:1, :] - lse) * out_recv[n, local].astype(F32)
            for n in range(n_ka)
        )
        att_ref[:, local * dim : (local + 1) * dim] = mixed.T.astype(BF16)
        dq_recv[panel, local] = (dq_acc[:, cols] * scale).astype(BF16)

    total = x_total(last)
    for k in range(last):
        z_sum_copy(k).wait_recv()
        total = total + z_recv[k].astype(F32)
    kg_ref[...] = total[0:chunk]
    vg_ref[...] = total[chunk : 2 * chunk]

    for local in range(own_heads):
        for s in range(1, n_ka):
            part_arrived(dq_recv, dq_send_sem, dq_recv_sem, ring(panel, s, n_ka), local)
        summed = sum(dq_recv[n, local].astype(F32) for n in range(n_ka))
        qg_ref[:, local * dim : (local + 1) * dim] = summed.T

    def drain_group(k, _):
        x_copy(k).wait_send()
        core_copy(k, 0).wait_send()
        core_copy(k, 1).wait_send()
        core_sum_copy(k).wait_send()
        x_sum_copy(k).wait_send()

        @pl.when(k < last)
        def _():
            z_copy(k + 1).wait_send()
            z_sum_copy(k).wait_send()

        return 0

    lax.fori_loop(0, groups, drain_group, 0)

    def drain_head(i, _):
        head = head_at(i)
        for s in range(1, n_ka):
            stat_copy(head, s).wait_send()

        @pl.when(foreign(head))
        def _():
            part_copy(out_send, out_recv, out_send_sem, out_recv_sem, head).wait_send()
            part_copy(dq_send, dq_recv, dq_send_sem, dq_recv_sem, head).wait_send()

        return 0

    lax.fori_loop(0, heads, drain_head, 0)


def hand_over(a, b, c, d, a_out, b_out, c_out, d_out, sem):
    pairs = ((a, a_out), (b, b_out), (c, c_out), (d, d_out))
    copies = [pltpu.make_async_copy(src, dst, sem.at[i]) for i, (src, dst) in enumerate(pairs)]
    for copy in copies:
        copy.start()
    for copy in copies:
        copy.wait()


def per_device(n_pb, n_ka, queries, keys, values, dout, block_mask):
    rows, width = queries.shape
    chunk, dim = keys.shape
    heads = width // dim
    own_heads = heads // n_ka
    groups = n_pb // 4
    group_keys = 4 * chunk
    wide = heads * rows
    assert rows == 2 * BLOCK and heads % 4 == 0 and group_keys % BLOCK == 0
    vmem, dma = pltpu.VMEM, pltpu.SemaphoreType.DMA
    pair = (2 * chunk, dim)
    results = pl.pallas_call(
        functools.partial(kernel, n_pb, n_ka),
        out_shape=(
            jax.ShapeDtypeStruct((rows, own_heads * dim), BF16),
            jax.ShapeDtypeStruct((rows, own_heads * dim), F32),
            jax.ShapeDtypeStruct((chunk, dim), F32),
            jax.ShapeDtypeStruct((chunk, dim), F32),
        ),
        in_specs=[pl.BlockSpec(memory_space=pltpu.SMEM)]
        + [pl.BlockSpec(memory_space=pl.ANY)] * 4,
        out_specs=[pl.BlockSpec(memory_space=pltpu.VMEM)] * 4,
        scratch_shapes=[
            vmem((n_pb,) + pair, BF16),
            vmem((groups, dim, group_keys), BF16),
            vmem((wide, dim), BF16),
            vmem((wide, dim), BF16),
            vmem((dim, wide), BF16),
            vmem((dim, wide), BF16),
            vmem((groups, group_keys, wide), BF16),
            vmem((heads // 4, group_keys, 2 * rows), F32),
            vmem((group_keys, wide), BF16),
            vmem((group_keys, wide), BF16),
            vmem((dim, wide), F32),
            vmem((dim, wide), F32),
            vmem((1, wide), F32),
            vmem((1, wide), F32),
            vmem((groups, 1, wide), F32),
            vmem((1, wide), F32),
            vmem((1, wide), F32),
            vmem((n_ka, heads, 8, rows), F32),
            vmem((heads, dim, rows), BF16),
            vmem((n_ka, own_heads, dim, rows), BF16),
            vmem((heads, dim, rows), BF16),
            vmem((n_ka, own_heads, dim, rows), BF16),
            vmem((groups, 4) + pair, F32),
            vmem((groups, 2) + pair, BF16),
            vmem((groups, 2) + pair, BF16),
            vmem((groups,) + pair, BF16),
            vmem((groups,) + pair, BF16),
            vmem((groups,) + pair, BF16),
            vmem((groups,) + pair, BF16),
            dma((2 + 2 * heads,)),
            dma((n_pb,)),
            dma((groups,)),
            dma((groups,)),
            dma((2 * groups,)),
            dma((heads, n_ka)),
            dma((n_ka, heads)),
            dma((heads,)),
            dma((n_ka, own_heads)),
            dma((heads,)),
            dma((n_ka, own_heads)),
            dma((groups,)),
            dma((groups,)),
            dma((groups,)),
            dma((groups,)),
            dma((groups,)),
            dma((groups,)),
        ],
        compiler_params=pltpu.CompilerParams(
            collective_id=0, has_side_effects=True, vmem_limit_bytes=58 * 2**20
        ),
        cost_estimate=pl.CostEstimate(
            flops=12 * wide * n_pb * chunk * dim,
            bytes_accessed=4 * rows * width * 2,
            transcendentals=wide * n_pb * chunk,
        ),
    )(block_mask, queries, keys, values, dout)
    return pl.pallas_call(
        hand_over,
        out_shape=tuple(jax.ShapeDtypeStruct(one.shape, one.dtype) for one in results),
        in_specs=[pl.BlockSpec(memory_space=pl.ANY)] * 4,
        out_specs=[pl.BlockSpec(memory_space=pltpu.VMEM)] * 4,
        scratch_shapes=[dma((4,))],
        compiler_params=pltpu.CompilerParams(vmem_limit_bytes=63 * 2**20),
    )(*results)


def solution(mesh):
    in_specs = (
        P("pb", None),
        P(("ka", "pb"), None),
        P(("ka", "pb"), None),
        P("pb", None),
        P("pb", "ka"),
    )
    out_specs = (P("pb", "ka"), P("pb", "ka"), P(("ka", "pb"), None), P(("ka", "pb"), None))
    return jax.shard_map(
        functools.partial(per_device, mesh.shape["pb"], mesh.shape["ka"]),
        mesh=mesh, in_specs=in_specs, out_specs=out_specs, check_vma=False,
    )
```

```python
import functools
import math

import jax
import jax.numpy as jnp
from jax import lax
from jax.experimental import pallas as pl
from jax.experimental.pallas import tpu as pltpu
from jax.sharding import PartitionSpec as P

BLOCK = 128
DEAD = 1e30
F32 = jnp.float32
BF16 = jnp.bfloat16


def dot_nn(a, b):
    return jnp.dot(a, b, preferred_element_type=F32)


def dot_nt(a, b):
    return lax.dot_general(a, b, (((1,), (1,)), ((), ())), preferred_element_type=F32)


def kernel(
    n_pb, n_ka,
    mask_ref, q_ref, k_ref, v_ref, do_ref,
    att_ref, qg_ref, kg_ref, vg_ref,
    kv, k_turned, q_rows, do_rows, q_turned, do_turned, weights, wide_scores, probs, dscores,
    out_acc, dq_acc, run_max, run_total, group_max, row_lse, row_delta,
    stat_recv, out_send, out_recv, dq_send, dq_recv,
    acc, core_send, core_recv, x_send, x_recv, z_send, z_recv,
    load_sem, ag_recv_sem, ag_z_sem, ag_x_sem, ag_core_sem,
    stat_send_sem, stat_recv_sem, out_send_sem, out_recv_sem, dq_send_sem, dq_recv_sem,
    core_send_sem, core_recv_sem, x_send_sem, x_recv_sem, z_send_sem, z_recv_sem,
):
    rows, width = q_ref.shape
    chunk, dim = k_ref.shape
    heads = width // dim
    own_heads = heads // n_ka
    groups = n_pb // 4
    group_keys = 4 * chunk
    group_blocks = group_keys // BLOCK
    scale = 1.0 / math.sqrt(dim)
    log_scale = scale * math.log2(math.e)

    me = lax.axis_index("pb")
    panel = lax.axis_index("ka")
    core = lax.rem(me, 2)
    x = lax.rem(me // 2, 2)
    z = me // 4
    other_core, other_x = 1 - core, 1 - x

    def at(z_index, x_index, core_index):
        return (z_index * 2 + x_index) * 2 + core_index

    core_peer, x_peer = at(z, x, other_core), at(z, other_x, core)

    def remote(src, dst, send_sem, recv_sem, device):
        return pltpu.make_async_remote_copy(
            src_ref=src, dst_ref=dst, send_sem=send_sem, recv_sem=recv_sem,
            device_id=device, device_id_type=pl.DeviceIdType.MESH,
        )

    def ring(start, step, size):
        return lax.rem(start + step, size)

    def load(index, src, dst):
        return pltpu.make_async_copy(src, dst, load_sem.at[index])

    loads = [
        load(0, k_ref, kv.at[me, pl.ds(0, chunk)]),
        load(1, v_ref, kv.at[me, pl.ds(chunk, chunk)]),
    ]
    for part, (src, dst) in enumerate(((q_ref, q_rows), (do_ref, do_rows))):
        for head in range(heads):
            loads.append(
                load(
                    2 + part * heads + head,
                    src.at[:, pl.ds(head * dim, dim)],
                    dst.at[pl.ds(head * rows, rows), :],
                )
            )
    for one in loads:
        one.start()

    barrier = pltpu.get_barrier_semaphore()
    partners = [{"pb": core_peer}, {"pb": x_peer}]
    partners += [{"pb": at(ring(z, s, groups), x, core)} for s in range(1, groups)]
    partners += [{"ka": ring(panel, s, n_ka)} for s in range(1, n_ka)]
    for partner in partners:
        pl.semaphore_signal(barrier, inc=1, device_id=partner, device_id_type=pl.DeviceIdType.MESH)
    loads[0].wait()
    loads[1].wait()
    pl.semaphore_wait(barrier, len(partners))

    def gather_copy(index, send_sem, device):
        return remote(kv.at[index], kv.at[index], send_sem, ag_recv_sem.at[index], {"pb": device})

    def z_copy(s):
        return gather_copy(me, ag_z_sem.at[s], at(ring(z, s, groups), x, core))

    def x_copy(k):
        return gather_copy(at(ring(z, k, groups), x, core), ag_x_sem.at[k], x_peer)

    def core_copy(k, part):
        owner_x = x if part == 0 else other_x
        index = at(ring(z, k, groups), owner_x, core)
        return gather_copy(index, ag_core_sem.at[2 * k + part], core_peer)

    def arrived(index):
        gather_copy(index, ag_x_sem.at[0], core_peer).wait_recv()

    x_copy(0).start()
    core_copy(0, 0).start()
    for s in range(1, groups):
        z_copy(s).start()

    def head_columns(head, count=1):
        return pl.ds(pl.multiple_of(head * rows, rows), count * rows)

    def head_at(i):
        return lax.rem((panel + 1) * own_heads + i, heads) if own_heads % 2 == 0 else i

    def foreign(head):
        return head // own_heads != panel

    out_acc[...] = jnp.zeros_like(out_acc)
    dq_acc[...] = jnp.zeros_like(dq_acc)
    run_max[...] = jnp.full_like(run_max, -1e38)
    run_total[...] = jnp.zeros_like(run_total)

    def stage_x(k):
        arrived(at(ring(z, k, groups), other_x, core))
        core_copy(k, 1).start()

    def stage_core(k):
        arrived(at(ring(z, k, groups), x, other_core))
        arrived(at(ring(z, k, groups), other_x, other_core))

    def turn(src, dst, first):
        for head in range(heads):
            loads[first + head].wait()
            span = pl.ds(head * rows, rows)
            dst[:, span] = src[span, :].T

    turn(q_rows, q_turned, 2)
    stage_x(0)
    turn(do_rows, do_turned, 2 + heads)
    stage_core(0)

    def group_rows(group, first):
        return kv[pl.ds(group * 4, 4), first : first + chunk, :].reshape(group_keys, dim)

    def stage_z(k):
        arrived(at(ring(z, k, groups), x, core))
        x_copy(k).start()
        core_copy(k, 0).start()

    def forward_group(k, middle=None):
        group = ring(z, k, groups)
        keys = group_rows(group, 0)
        k_turned[group] = keys.T
        values_turned = group_rows(group, chunk).T
        bias = [
            (mask_ref[0, group * group_blocks + b].astype(F32) - 1.0) * DEAD
            for b in range(group_blocks)
        ]

        def forward_heads(first, last):
            def score(i):
                scores = dot_nn(group_rows(group, 0), q_turned[:, head_columns(head_at(i), 2)])
                wide_scores[(i - first) // 2] = scores
                return [
                    jnp.max(scores[b * BLOCK : (b + 1) * BLOCK], axis=0, keepdims=True) * log_scale
                    for b in range(group_blocks)
                ]

            peaks = score(first)
            for i in range(first, last, 2):
                later = score(i + 2) if i + 2 < last else None
                cols = head_columns(head_at(i), 2)
                peak = functools.reduce(jnp.maximum, [p + one for p, one in zip(peaks, bias)])
                low = []
                total = jnp.zeros_like(peak)
                for b in range(group_blocks):
                    shift = jnp.maximum(peak - bias[b], peaks[b])
                    part = wide_scores[(i - first) // 2, b * BLOCK : (b + 1) * BLOCK, :]
                    weight = jnp.exp2(part * log_scale - shift)
                    total = total + jnp.sum(weight, axis=0, keepdims=True)
                    low.append(weight.astype(BF16))
                low = jnp.concatenate(low, axis=0)
                weights[group, :, cols] = low
                group_max[group, :, cols] = peak
                old = run_max[:, cols]
                new = jnp.maximum(old, peak)
                keep, add = jnp.exp2(old - new), jnp.exp2(peak - new)
                run_max[:, cols] = new
                run_total[:, cols] = run_total[:, cols] * keep + total * add
                out_acc[:, cols] = out_acc[:, cols] * keep + dot_nn(values_turned, low) * add
                peaks = later

        if middle is None:
            forward_heads(0, heads)
        else:
            forward_heads(0, heads // 2)
            middle()
            forward_heads(heads // 2, heads)

    def later_group(k, _):
        @pl.when(k + 2 < groups)
        def _():
            stage_z(k + 2)

        @pl.when(k + 1 < groups)
        def _():
            stage_x(k + 1)

        forward_group(k)

        @pl.when(k + 1 < groups)
        def _():
            stage_core(k + 1)

        return 0

    for k in range(1, min(3, groups)):
        stage_z(k)
    if groups > 1:
        forward_group(0, lambda: stage_x(1))
        stage_core(1)
        lax.fori_loop(1, groups, later_group, 0)
    else:
        forward_group(0)

    def stat_copy(head, s):
        return remote(
            stat_recv.at[panel, head], stat_recv.at[panel, head],
            stat_send_sem.at[head, s], stat_recv_sem.at[panel, head],
            {"ka": ring(panel, s, n_ka)},
        )

    def stat_arrived(head, source):
        remote(
            stat_recv.at[source, head], stat_recv.at[source, head],
            stat_send_sem.at[head, 0], stat_recv_sem.at[source, head],
            {"ka": ring(panel, 1, n_ka)},
        ).wait_recv()

    def part_copy(send, recv, send_sem, recv_sem, head):
        local = lax.rem(head, own_heads)
        return remote(
            send.at[head], recv.at[panel, local], send_sem.at[head], recv_sem.at[panel, local],
            {"ka": head // own_heads},
        )

    def part_arrived(recv, send_sem, recv_sem, source, local):
        remote(
            recv.at[source, local], recv.at[source, local],
            send_sem.at[0], recv_sem.at[source, local], {"ka": ring(panel, 1, n_ka)},
        ).wait_recv()

    def finish_stats(i, _):
        head = head_at(i)
        cols = head_columns(head)
        total = run_total[:, cols]
        delta = jnp.sum(out_acc[:, cols] * do_turned[:, cols].astype(F32), axis=0, keepdims=True)
        stat_recv[panel, head, 0:1, :] = run_max[:, cols] + jnp.log2(total)
        stat_recv[panel, head, 1:2, :] = delta / total
        for s in range(1, n_ka):
            stat_copy(head, s).start()
        return 0

    def finish_out(i, _):
        head = head_at(i)
        cols = head_columns(head)
        out = (out_acc[:, cols] * (1.0 / run_total[:, cols])).astype(BF16)

        @pl.when(foreign(head))
        def _():
            out_send[head] = out
            part_copy(out_send, out_recv, out_send_sem, out_recv_sem, head).start()

        @pl.when(jnp.logical_not(foreign(head)))
        def _():
            out_recv[panel, lax.rem(head, own_heads)] = out

        return 0

    lax.fori_loop(0, heads, finish_stats, 0)
    lax.fori_loop(0, heads, finish_out, 0)

    def merge_head(i, _):
        head = head_at(i)
        cols = head_columns(head)
        for s in range(1, n_ka):
            stat_arrived(head, ring(panel, s, n_ka))
        lses = [stat_recv[n, head, 0:1, :] for n in range(n_ka)]
        peak = functools.reduce(jnp.maximum, lses)
        lse = peak + jnp.log2(sum(jnp.exp2(one - peak) for one in lses))
        row_lse[:, cols] = lse
        row_delta[:, cols] = sum(
            jnp.exp2(lses[n] - lse) * stat_recv[n, head, 1:2, :] for n in range(n_ka)
        )
        return 0

    half = heads // 2
    lax.fori_loop(0, half, merge_head, 0)

    def back_group_of(k):
        return ring(z, k + 1, groups)

    def core_sum_copy(k):
        return remote(
            core_send.at[k], core_recv.at[k], core_send_sem.at[k], core_recv_sem.at[k],
            {"pb": core_peer},
        )

    def x_sum_copy(k):
        return remote(
            x_send.at[k], x_recv.at[k], x_send_sem.at[k], x_recv_sem.at[k], {"pb": x_peer}
        )

    def z_sum_copy(k):
        return remote(
            z_send.at[k], z_recv.at[k], z_send_sem.at[k], z_recv_sem.at[k],
            {"pb": at(back_group_of(k), x, core)},
        )

    def send_core(k):
        for part in range(2):
            core_send[k, part] = acc[k, 2 * part + other_core].astype(BF16)
        core_sum_copy(k).start()

    def send_x(k):
        core_sum_copy(k).wait_recv()
        passed = acc[k, 2 * other_x + core] + core_recv[k, other_x].astype(F32)
        x_send[k] = passed.astype(BF16)
        x_sum_copy(k).start()
        mine = 2 * x + core
        acc[k, mine] = acc[k, mine] + core_recv[k, x].astype(F32)

    def x_total(k):
        x_sum_copy(k).wait_recv()
        return acc[k, 2 * x + core] + x_recv[k].astype(F32)

    def send_z(k):
        z_send[k] = x_total(k).astype(BF16)
        z_sum_copy(k).start()

    def backward_block(k, first, last, middle=lambda: None):
        group = back_group_of(k)
        sums = []

        def rows_of(i):
            return pl.ds(pl.multiple_of(head_at(i) * rows, rows), 2 * rows)

        def products(i):
            cols = head_columns(head_at(i), 2)
            place = slice(i * rows, (i + 2) * rows)
            dq_acc[:, cols] = dq_acc[:, cols] + dot_nn(k_turned[group], dscores[:, place])
            sums.append(
                (
                    dot_nn(dscores[:, place], q_rows[rows_of(i), :]),
                    dot_nn(probs[:, place], do_rows[rows_of(i), :]),
                )
            )

        for i in range(first, last, 2):
            cols = head_columns(head_at(i), 2)
            place = slice(i * rows, (i + 2) * rows)
            mix = jnp.exp2(group_max[group, :, cols] - row_lse[:, cols])
            dprobs = dot_nn(group_rows(group, chunk), do_turned[:, cols])
            if i > first:
                products(i - 2)
            low = weights[group, :, cols] * mix.astype(BF16)
            probs[:, place] = low
            dscores[:, place] = low * (dprobs - row_delta[:, cols]).astype(BF16)
        middle()
        products(last - 2)
        key_part = sum(one[0] for one in sums) * scale
        value_part = sum(one[1] for one in sums)
        return key_part.reshape(4, chunk, dim), value_part.reshape(4, chunk, dim)

    def send_dq(i, _):
        head = head_at(i)

        @pl.when(foreign(head))
        def _():
            dq_send[head] = (dq_acc[:, head_columns(head)] * scale).astype(BF16)
            part_copy(dq_send, dq_recv, dq_send_sem, dq_recv_sem, head).start()

        return 0

    def sweep_one(k, _):
        key_part, value_part = backward_block(k, 0, half)
        acc[k, :, 0:chunk, :] = key_part
        acc[k, :, chunk : 2 * chunk, :] = value_part
        return 0

    def sweep_two(k, _):
        def middle():
            @pl.when(k > 0)
            def _():
                send_x(k - 1)

            @pl.when(k > 1)
            def _():
                send_z(k - 2)

        key_part, value_part = backward_block(k, half, heads, middle)
        acc[k, :, 0:chunk, :] = acc[k, :, 0:chunk, :] + key_part
        acc[k, :, chunk : 2 * chunk, :] = acc[k, :, chunk : 2 * chunk, :] + value_part
        send_core(k)
        return 0

    lax.fori_loop(0, groups, sweep_one, 0, unroll=2)
    lax.fori_loop(0, half, send_dq, 0)
    lax.fori_loop(half, heads, merge_head, 0)
    lax.fori_loop(0, groups, sweep_two, 0)
    lax.fori_loop(half, heads, send_dq, 0)
    last = groups - 1
    if groups > 1:
        send_z(last - 1)
    send_x(last)

    for local in range(own_heads):
        head = panel * own_heads + local
        cols = head_columns(head)
        for s in range(1, n_ka):
            part_arrived(out_recv, out_send_sem, out_recv_sem, ring(panel, s, n_ka), local)
        lse = row_lse[:, cols]
        mixed = sum(
            jnp.exp2(stat_recv[n, head, 0:1, :] - lse) * out_recv[n, local].astype(F32)
            for n in range(n_ka)
        )
        att_ref[:, local * dim : (local + 1) * dim] = mixed.T.astype(BF16)
        dq_recv[panel, local] = (dq_acc[:, cols] * scale).astype(BF16)

    total = x_total(last)
    for k in range(last):
        z_sum_copy(k).wait_recv()
        total = total + z_recv[k].astype(F32)
    kg_ref[...] = total[0:chunk]
    vg_ref[...] = total[chunk : 2 * chunk]

    for local in range(own_heads):
        for s in range(1, n_ka):
            part_arrived(dq_recv, dq_send_sem, dq_recv_sem, ring(panel, s, n_ka), local)
        summed = sum(dq_recv[n, local].astype(F32) for n in range(n_ka))
        qg_ref[:, local * dim : (local + 1) * dim] = summed.T

    def drain_group(k, _):
        x_copy(k).wait_send()
        core_copy(k, 0).wait_send()
        core_copy(k, 1).wait_send()
        core_sum_copy(k).wait_send()
        x_sum_copy(k).wait_send()

        @pl.when(k < last)
        def _():
            z_copy(k + 1).wait_send()
            z_sum_copy(k).wait_send()

        return 0

    lax.fori_loop(0, groups, drain_group, 0)

    def drain_head(i, _):
        head = head_at(i)
        for s in range(1, n_ka):
            stat_copy(head, s).wait_send()

        @pl.when(foreign(head))
        def _():
            part_copy(out_send, out_recv, out_send_sem, out_recv_sem, head).wait_send()
            part_copy(dq_send, dq_recv, dq_send_sem, dq_recv_sem, head).wait_send()

        return 0

    lax.fori_loop(0, heads, drain_head, 0)


def hand_over(a, b, c, d, a_out, b_out, c_out, d_out, sem):
    pairs = ((a, a_out), (b, b_out), (c, c_out), (d, d_out))
    copies = [pltpu.make_async_copy(src, dst, sem.at[i]) for i, (src, dst) in enumerate(pairs)]
    for copy in copies:
        copy.start()
    for copy in copies:
        copy.wait()


def per_device(n_pb, n_ka, queries, keys, values, dout, block_mask):
    rows, width = queries.shape
    chunk, dim = keys.shape
    heads = width // dim
    own_heads = heads // n_ka
    groups = n_pb // 4
    group_keys = 4 * chunk
    wide = heads * rows
    assert rows == 2 * BLOCK and heads % 4 == 0 and group_keys % BLOCK == 0
    vmem, dma = pltpu.VMEM, pltpu.SemaphoreType.DMA
    pair = (2 * chunk, dim)
    results = pl.pallas_call(
        functools.partial(kernel, n_pb, n_ka),
        out_shape=(
            jax.ShapeDtypeStruct((rows, own_heads * dim), BF16),
            jax.ShapeDtypeStruct((rows, own_heads * dim), F32),
            jax.ShapeDtypeStruct((chunk, dim), F32),
            jax.ShapeDtypeStruct((chunk, dim), F32),
        ),
        in_specs=[pl.BlockSpec(memory_space=pltpu.SMEM)]
        + [pl.BlockSpec(memory_space=pl.ANY)] * 4,
        out_specs=[pl.BlockSpec(memory_space=pltpu.VMEM)] * 4,
        scratch_shapes=[
            vmem((n_pb,) + pair, BF16),
            vmem((groups, dim, group_keys), BF16),
            vmem((wide, dim), BF16),
            vmem((wide, dim), BF16),
            vmem((dim, wide), BF16),
            vmem((dim, wide), BF16),
            vmem((groups, group_keys, wide), BF16),
            vmem((heads // 2, group_keys, 2 * rows), F32),
            vmem((group_keys, wide), BF16),
            vmem((group_keys, wide), BF16),
            vmem((dim, wide), F32),
            vmem((dim, wide), F32),
            vmem((1, wide), F32),
            vmem((1, wide), F32),
            vmem((groups, 1, wide), F32),
            vmem((1, wide), F32),
            vmem((1, wide), F32),
            vmem((n_ka, heads, 8, rows), F32),
            vmem((heads, dim, rows), BF16),
            vmem((n_ka, own_heads, dim, rows), BF16),
            vmem((heads, dim, rows), BF16),
            vmem((n_ka, own_heads, dim, rows), BF16),
            vmem((groups, 4) + pair, F32),
            vmem((groups, 2) + pair, BF16),
            vmem((groups, 2) + pair, BF16),
            vmem((groups,) + pair, BF16),
            vmem((groups,) + pair, BF16),
            vmem((groups,) + pair, BF16),
            vmem((groups,) + pair, BF16),
            dma((2 + 2 * heads,)),
            dma((n_pb,)),
            dma((groups,)),
            dma((groups,)),
            dma((2 * groups,)),
            dma((heads, n_ka)),
            dma((n_ka, heads)),
            dma((heads,)),
            dma((n_ka, own_heads)),
            dma((heads,)),
            dma((n_ka, own_heads)),
            dma((groups,)),
            dma((groups,)),
            dma((groups,)),
            dma((groups,)),
            dma((groups,)),
            dma((groups,)),
        ],
        compiler_params=pltpu.CompilerParams(
            collective_id=0, has_side_effects=True, vmem_limit_bytes=58 * 2**20
        ),
        cost_estimate=pl.CostEstimate(
            flops=12 * wide * n_pb * chunk * dim,
            bytes_accessed=4 * rows * width * 2,
            transcendentals=wide * n_pb * chunk,
        ),
    )(block_mask, queries, keys, values, dout)
    return pl.pallas_call(
        hand_over,
        out_shape=tuple(jax.ShapeDtypeStruct(one.shape, one.dtype) for one in results),
        in_specs=[pl.BlockSpec(memory_space=pl.ANY)] * 4,
        out_specs=[pl.BlockSpec(memory_space=pltpu.VMEM)] * 4,
        scratch_shapes=[dma((4,))],
        compiler_params=pltpu.CompilerParams(vmem_limit_bytes=63 * 2**20),
    )(*results)


def solution(mesh):
    in_specs = (
        P("pb", None),
        P(("ka", "pb"), None),
        P(("ka", "pb"), None),
        P("pb", None),
        P("pb", "ka"),
    )
    out_specs = (P("pb", "ka"), P("pb", "ka"), P(("ka", "pb"), None), P(("ka", "pb"), None))
    return jax.shard_map(
        functools.partial(per_device, mesh.shape["pb"], mesh.shape["ka"]),
        mesh=mesh, in_specs=in_specs, out_specs=out_specs, check_vma=False,
    )
```

```python
import functools
import math

import jax
import jax.numpy as jnp
from jax import lax
from jax.experimental import pallas as pl
from jax.experimental.pallas import tpu as pltpu
from jax.sharding import PartitionSpec as P

BLOCK = 128
DEAD = 1e30
F32 = jnp.float32
BF16 = jnp.bfloat16


def dot_nn(a, b):
    return jnp.dot(a, b, preferred_element_type=F32)


def dot_nt(a, b):
    return lax.dot_general(a, b, (((1,), (1,)), ((), ())), preferred_element_type=F32)


def kernel(
    n_pb, n_ka,
    mask_ref, q_ref, k_ref, v_ref, do_ref,
    att_ref, qg_ref, kg_ref, vg_ref,
    kv, k_turned, q_rows, do_rows, q_turned, do_turned, weights, wide_scores, probs, dscores,
    out_acc, dq_acc, run_max, run_total, group_max, row_lse, row_delta,
    stat_recv, out_send, out_recv, dq_send, dq_recv,
    acc, core_send, core_recv, x_send, x_recv, z_send, z_recv,
    load_sem, ag_recv_sem, ag_z_sem, ag_x_sem, ag_core_sem,
    stat_send_sem, stat_recv_sem, out_send_sem, out_recv_sem, dq_send_sem, dq_recv_sem,
    core_send_sem, core_recv_sem, x_send_sem, x_recv_sem, z_send_sem, z_recv_sem,
):
    rows, width = q_ref.shape
    chunk, dim = k_ref.shape
    heads = width // dim
    own_heads = heads // n_ka
    groups = n_pb // 4
    group_keys = 4 * chunk
    group_blocks = group_keys // BLOCK
    scale = 1.0 / math.sqrt(dim)
    log_scale = scale * math.log2(math.e)

    me = lax.axis_index("pb")
    panel = lax.axis_index("ka")
    core = lax.rem(me, 2)
    x = lax.rem(me // 2, 2)
    z = me // 4
    other_core, other_x = 1 - core, 1 - x

    def at(z_index, x_index, core_index):
        return (z_index * 2 + x_index) * 2 + core_index

    core_peer, x_peer = at(z, x, other_core), at(z, other_x, core)

    def remote(src, dst, send_sem, recv_sem, device):
        return pltpu.make_async_remote_copy(
            src_ref=src, dst_ref=dst, send_sem=send_sem, recv_sem=recv_sem,
            device_id=device, device_id_type=pl.DeviceIdType.MESH,
        )

    def ring(start, step, size):
        return lax.rem(start + step, size)

    def load(index, src, dst):
        return pltpu.make_async_copy(src, dst, load_sem.at[index])

    loads = [
        load(0, k_ref, kv.at[me, pl.ds(0, chunk)]),
        load(1, v_ref, kv.at[me, pl.ds(chunk, chunk)]),
    ]
    for part, (src, dst) in enumerate(((q_ref, q_rows), (do_ref, do_rows))):
        for head in range(heads):
            loads.append(
                load(
                    2 + part * heads + head,
                    src.at[:, pl.ds(head * dim, dim)],
                    dst.at[pl.ds(head * rows, rows), :],
                )
            )
    for one in loads:
        one.start()

    barrier = pltpu.get_barrier_semaphore()
    partners = [{"pb": core_peer}, {"pb": x_peer}]
    partners += [{"pb": at(ring(z, s, groups), x, core)} for s in range(1, groups)]
    partners += [{"ka": ring(panel, s, n_ka)} for s in range(1, n_ka)]
    for partner in partners:
        pl.semaphore_signal(barrier, inc=1, device_id=partner, device_id_type=pl.DeviceIdType.MESH)
    loads[0].wait()
    loads[1].wait()
    pl.semaphore_wait(barrier, len(partners))

    def gather_copy(index, send_sem, device):
        return remote(kv.at[index], kv.at[index], send_sem, ag_recv_sem.at[index], {"pb": device})

    def z_copy(s):
        return gather_copy(me, ag_z_sem.at[s], at(ring(z, s, groups), x, core))

    def x_copy(k):
        return gather_copy(at(ring(z, k, groups), x, core), ag_x_sem.at[k], x_peer)

    def core_copy(k, part):
        owner_x = x if part == 0 else other_x
        index = at(ring(z, k, groups), owner_x, core)
        return gather_copy(index, ag_core_sem.at[2 * k + part], core_peer)

    def arrived(index):
        gather_copy(index, ag_x_sem.at[0], core_peer).wait_recv()

    x_copy(0).start()
    core_copy(0, 0).start()
    for s in range(1, groups):
        z_copy(s).start()

    def head_columns(head, count=1):
        return pl.ds(pl.multiple_of(head * rows, rows), count * rows)

    def head_at(i):
        return lax.rem((panel + 1) * own_heads + i, heads) if own_heads % 2 == 0 else i

    def foreign(head):
        return head // own_heads != panel

    out_acc[...] = jnp.zeros_like(out_acc)
    dq_acc[...] = jnp.zeros_like(dq_acc)
    run_max[...] = jnp.full_like(run_max, -1e38)
    run_total[...] = jnp.zeros_like(run_total)

    def stage_x(k):
        arrived(at(ring(z, k, groups), other_x, core))
        core_copy(k, 1).start()

    def stage_core(k):
        arrived(at(ring(z, k, groups), x, other_core))
        arrived(at(ring(z, k, groups), other_x, other_core))

    def turn(src, dst, first):
        for head in range(heads):
            loads[first + head].wait()
            span = pl.ds(head * rows, rows)
            dst[:, span] = src[span, :].T

    turn(q_rows, q_turned, 2)
    stage_x(0)
    turn(do_rows, do_turned, 2 + heads)
    stage_core(0)

    def group_rows(group, first):
        return kv[pl.ds(group * 4, 4), first : first + chunk, :].reshape(group_keys, dim)

    def stage_z(k):
        arrived(at(ring(z, k, groups), x, core))
        x_copy(k).start()
        core_copy(k, 0).start()

    def forward_group(k, middle=None):
        group = ring(z, k, groups)
        keys = group_rows(group, 0)
        k_turned[group] = keys.T
        values_turned = jnp.concatenate(
            [group_rows(group, chunk).T, jnp.ones((16, group_keys), BF16)], axis=0
        )
        bias = [
            (mask_ref[0, group * group_blocks + b].astype(F32) - 1.0) * DEAD
            for b in range(group_blocks)
        ]

        def forward_heads(first, last):
            def score(i):
                scores = dot_nn(group_rows(group, 0), q_turned[:, head_columns(head_at(i), 2)])
                wide_scores[(i - first) // 2] = scores
                return [
                    jnp.max(scores[b * BLOCK : (b + 1) * BLOCK], axis=0, keepdims=True) * log_scale
                    for b in range(group_blocks)
                ]

            peaks = score(first)
            for i in range(first, last, 2):
                later = score(i + 2) if i + 2 < last else None
                cols = head_columns(head_at(i), 2)
                peak = functools.reduce(jnp.maximum, [p + one for p, one in zip(peaks, bias)])
                low = []
                for b in range(group_blocks):
                    shift = jnp.maximum(peak - bias[b], peaks[b])
                    part = wide_scores[(i - first) // 2, b * BLOCK : (b + 1) * BLOCK, :]
                    weight = jnp.exp2(part * log_scale - shift)
                    low.append(weight.astype(BF16))
                low = jnp.concatenate(low, axis=0)
                weights[group, :, cols] = low
                group_max[group, :, cols] = peak
                old = run_max[:, cols]
                new = jnp.maximum(old, peak)
                keep, add = jnp.exp2(old - new), jnp.exp2(peak - new)
                run_max[:, cols] = new
                product = dot_nn(values_turned, low)
                total = product[dim : dim + 1]
                run_total[:, cols] = run_total[:, cols] * keep + total * add
                out_acc[:, cols] = out_acc[:, cols] * keep + product[0:dim] * add
                peaks = later

        if middle is None:
            forward_heads(0, heads)
        else:
            forward_heads(0, heads // 2)
            middle()
            forward_heads(heads // 2, heads)

    def later_group(k, _):
        @pl.when(k + 2 < groups)
        def _():
            stage_z(k + 2)

        @pl.when(k + 1 < groups)
        def _():
            stage_x(k + 1)

        forward_group(k)

        @pl.when(k + 1 < groups)
        def _():
            stage_core(k + 1)

        return 0

    def first_middle():
        stage_x(1)
        if groups > 2:
            stage_z(2)

    if groups > 1:
        stage_z(1)
        forward_group(0, first_middle)
        stage_core(1)
        lax.fori_loop(1, groups, later_group, 0)
    else:
        forward_group(0)

    def stat_copy(s):
        return remote(
            stat_recv.at[panel], stat_recv.at[panel],
            stat_send_sem.at[s], stat_recv_sem.at[panel], {"ka": ring(panel, s, n_ka)},
        )

    def stat_arrived(source):
        remote(
            stat_recv.at[source], stat_recv.at[source],
            stat_send_sem.at[0], stat_recv_sem.at[source], {"ka": ring(panel, 1, n_ka)},
        ).wait_recv()

    def part_copy(send, recv, send_sem, recv_sem, head):
        local = lax.rem(head, own_heads)
        return remote(
            send.at[head], recv.at[panel, local], send_sem.at[head], recv_sem.at[panel, local],
            {"ka": head // own_heads},
        )

    def part_arrived(recv, send_sem, recv_sem, source, local):
        remote(
            recv.at[source, local], recv.at[source, local],
            send_sem.at[0], recv_sem.at[source, local], {"ka": ring(panel, 1, n_ka)},
        ).wait_recv()

    totals = run_total[...]
    deltas = jnp.sum(out_acc[...] * do_turned[...].astype(F32), axis=0, keepdims=True)
    stat_recv[panel, 0:1, :] = run_max[...] + jnp.log2(totals)
    stat_recv[panel, 1:2, :] = deltas / totals
    for s in range(1, n_ka):
        stat_copy(s).start()

    def finish_out(i, _):
        head = head_at(i)
        cols = head_columns(head)
        out = (out_acc[:, cols] * (1.0 / run_total[:, cols])).astype(BF16)

        @pl.when(foreign(head))
        def _():
            out_send[head] = out
            part_copy(out_send, out_recv, out_send_sem, out_recv_sem, head).start()

        @pl.when(jnp.logical_not(foreign(head)))
        def _():
            out_recv[panel, lax.rem(head, own_heads)] = out

        return 0

    lax.fori_loop(0, heads, finish_out, 0, unroll=2)

    for s in range(1, n_ka):
        stat_arrived(ring(panel, s, n_ka))
    lses = [stat_recv[n, 0:1, :] for n in range(n_ka)]
    peak = functools.reduce(jnp.maximum, lses)
    lse = peak + jnp.log2(sum(jnp.exp2(one - peak) for one in lses))
    row_lse[...] = lse
    row_delta[...] = sum(jnp.exp2(lses[n] - lse) * stat_recv[n, 1:2, :] for n in range(n_ka))
    half = heads // 2

    def back_group_of(k):
        return ring(z, k + 1, groups)

    def core_sum_copy(k):
        return remote(
            core_send.at[k], core_recv.at[k], core_send_sem.at[k], core_recv_sem.at[k],
            {"pb": core_peer},
        )

    def x_sum_copy(k):
        return remote(
            x_send.at[k], x_recv.at[k], x_send_sem.at[k], x_recv_sem.at[k], {"pb": x_peer}
        )

    def z_sum_copy(k):
        return remote(
            z_send.at[k], z_recv.at[k], z_send_sem.at[k], z_recv_sem.at[k],
            {"pb": at(back_group_of(k), x, core)},
        )

    def send_core(k):
        for part in range(2):
            core_send[k, part] = acc[k, 2 * part + other_core].astype(BF16)
        core_sum_copy(k).start()

    def send_x(k):
        core_sum_copy(k).wait_recv()
        passed = acc[k, 2 * other_x + core] + core_recv[k, other_x].astype(F32)
        x_send[k] = passed.astype(BF16)
        x_sum_copy(k).start()
        mine = 2 * x + core
        acc[k, mine] = acc[k, mine] + core_recv[k, x].astype(F32)

    def x_total(k):
        x_sum_copy(k).wait_recv()
        return acc[k, 2 * x + core] + x_recv[k].astype(F32)

    def send_z(k):
        z_send[k] = x_total(k).astype(BF16)
        z_sum_copy(k).start()

    def backward_block(k, first, last, middle=lambda: None):
        group = back_group_of(k)
        sums = []

        def rows_of(i):
            return pl.ds(pl.multiple_of(head_at(i) * rows, rows), 2 * rows)

        def products(i):
            cols = head_columns(head_at(i), 2)
            place = slice(i * rows, (i + 2) * rows)
            dq_acc[:, cols] = dq_acc[:, cols] + dot_nn(k_turned[group], dscores[:, place])
            sums.append(
                (
                    dot_nn(dscores[:, place], q_rows[rows_of(i), :]),
                    dot_nn(probs[:, place], do_rows[rows_of(i), :]),
                )
            )

        for i in range(first, last, 2):
            cols = head_columns(head_at(i), 2)
            place = slice(i * rows, (i + 2) * rows)
            mix = jnp.exp2(group_max[group, :, cols] - row_lse[:, cols])
            dprobs = dot_nn(group_rows(group, chunk), do_turned[:, cols])
            if i > first:
                products(i - 2)
            low = weights[group, :, cols] * mix.astype(BF16)
            probs[:, place] = low
            dscores[:, place] = low * (dprobs - row_delta[:, cols]).astype(BF16)
        middle()
        products(last - 2)
        key_part = sum(one[0] for one in sums) * scale
        value_part = sum(one[1] for one in sums)
        return key_part.reshape(4, chunk, dim), value_part.reshape(4, chunk, dim)

    def send_dq(i, _):
        head = head_at(i)

        @pl.when(foreign(head))
        def _():
            dq_send[head] = (dq_acc[:, head_columns(head)] * scale).astype(BF16)
            part_copy(dq_send, dq_recv, dq_send_sem, dq_recv_sem, head).start()

        return 0

    def sweep_one(k, _):
        key_part, value_part = backward_block(k, 0, half)
        acc[k, :, 0:chunk, :] = key_part
        acc[k, :, chunk : 2 * chunk, :] = value_part
        return 0

    def sweep_two(k, _):
        def middle():
            @pl.when(k > 0)
            def _():
                send_x(k - 1)

            @pl.when(k > 1)
            def _():
                send_z(k - 2)

        key_part, value_part = backward_block(k, half, heads, middle)
        acc[k, :, 0:chunk, :] = acc[k, :, 0:chunk, :] + key_part
        acc[k, :, chunk : 2 * chunk, :] = acc[k, :, chunk : 2 * chunk, :] + value_part
        send_core(k)
        return 0

    lax.fori_loop(0, groups, sweep_one, 0, unroll=2)
    lax.fori_loop(0, half, send_dq, 0)
    lax.fori_loop(0, groups, sweep_two, 0)
    lax.fori_loop(half, heads, send_dq, 0)
    last = groups - 1
    if groups > 1:
        send_z(last - 1)
    send_x(last)

    for local in range(own_heads):
        head = panel * own_heads + local
        cols = head_columns(head)
        for s in range(1, n_ka):
            part_arrived(out_recv, out_send_sem, out_recv_sem, ring(panel, s, n_ka), local)
        lse = row_lse[:, cols]
        mixed = sum(
            jnp.exp2(stat_recv[n, 0:1, cols] - lse) * out_recv[n, local].astype(F32)
            for n in range(n_ka)
        )
        att_ref[:, local * dim : (local + 1) * dim] = mixed.T.astype(BF16)
        dq_recv[panel, local] = (dq_acc[:, cols] * scale).astype(BF16)

    for local in range(own_heads):
        for s in range(1, n_ka):
            part_arrived(dq_recv, dq_send_sem, dq_recv_sem, ring(panel, s, n_ka), local)
        summed = sum(dq_recv[n, local].astype(F32) for n in range(n_ka))
        qg_ref[:, local * dim : (local + 1) * dim] = summed.T

    total = x_total(last)
    for k in range(last):
        z_sum_copy(k).wait_recv()
        total = total + z_recv[k].astype(F32)
    kg_ref[...] = total[0:chunk]
    vg_ref[...] = total[chunk : 2 * chunk]

    def drain_group(k, _):
        x_copy(k).wait_send()
        core_copy(k, 0).wait_send()
        core_copy(k, 1).wait_send()
        core_sum_copy(k).wait_send()
        x_sum_copy(k).wait_send()

        @pl.when(k < last)
        def _():
            z_copy(k + 1).wait_send()
            z_sum_copy(k).wait_send()

        return 0

    lax.fori_loop(0, groups, drain_group, 0)

    def drain_head(i, _):
        head = head_at(i)
        @pl.when(foreign(head))
        def _():
            part_copy(out_send, out_recv, out_send_sem, out_recv_sem, head).wait_send()
            part_copy(dq_send, dq_recv, dq_send_sem, dq_recv_sem, head).wait_send()

        return 0

    lax.fori_loop(0, heads, drain_head, 0)
    for s in range(1, n_ka):
        stat_copy(s).wait_send()


def hand_over(a, b, c, d, a_out, b_out, c_out, d_out, sem):
    pairs = ((a, a_out), (b, b_out), (c, c_out), (d, d_out))
    copies = [pltpu.make_async_copy(src, dst, sem.at[i]) for i, (src, dst) in enumerate(pairs)]
    for copy in copies:
        copy.start()
    for copy in copies:
        copy.wait()


def per_device(n_pb, n_ka, queries, keys, values, dout, block_mask):
    rows, width = queries.shape
    chunk, dim = keys.shape
    heads = width // dim
    own_heads = heads // n_ka
    groups = n_pb // 4
    group_keys = 4 * chunk
    wide = heads * rows
    assert rows == 2 * BLOCK and heads % 4 == 0 and group_keys % BLOCK == 0
    vmem, dma = pltpu.VMEM, pltpu.SemaphoreType.DMA
    pair = (2 * chunk, dim)
    results = pl.pallas_call(
        functools.partial(kernel, n_pb, n_ka),
        out_shape=(
            jax.ShapeDtypeStruct((rows, own_heads * dim), BF16),
            jax.ShapeDtypeStruct((rows, own_heads * dim), F32),
            jax.ShapeDtypeStruct((chunk, dim), F32),
            jax.ShapeDtypeStruct((chunk, dim), F32),
        ),
        in_specs=[pl.BlockSpec(memory_space=pltpu.SMEM)]
        + [pl.BlockSpec(memory_space=pl.ANY)] * 4,
        out_specs=[pl.BlockSpec(memory_space=pltpu.VMEM)] * 4,
        scratch_shapes=[
            vmem((n_pb,) + pair, BF16),
            vmem((groups, dim, group_keys), BF16),
            vmem((wide, dim), BF16),
            vmem((wide, dim), BF16),
            vmem((dim, wide), BF16),
            vmem((dim, wide), BF16),
            vmem((groups, group_keys, wide), BF16),
            vmem((heads // 2, group_keys, 2 * rows), F32),
            vmem((group_keys, wide), BF16),
            vmem((group_keys, wide), BF16),
            vmem((dim, wide), F32),
            vmem((dim, wide), F32),
            vmem((1, wide), F32),
            vmem((1, wide), F32),
            vmem((groups, 1, wide), F32),
            vmem((1, wide), F32),
            vmem((1, wide), F32),
            vmem((n_ka, 2, wide), F32),
            vmem((heads, dim, rows), BF16),
            vmem((n_ka, own_heads, dim, rows), BF16),
            vmem((heads, dim, rows), BF16),
            vmem((n_ka, own_heads, dim, rows), BF16),
            vmem((groups, 4) + pair, F32),
            vmem((groups, 2) + pair, BF16),
            vmem((groups, 2) + pair, BF16),
            vmem((groups,) + pair, BF16),
            vmem((groups,) + pair, BF16),
            vmem((groups,) + pair, BF16),
            vmem((groups,) + pair, BF16),
            dma((2 + 2 * heads,)),
            dma((n_pb,)),
            dma((groups,)),
            dma((groups,)),
            dma((2 * groups,)),
            dma((n_ka,)),
            dma((n_ka,)),
            dma((heads,)),
            dma((n_ka, own_heads)),
            dma((heads,)),
            dma((n_ka, own_heads)),
            dma((groups,)),
            dma((groups,)),
            dma((groups,)),
            dma((groups,)),
            dma((groups,)),
            dma((groups,)),
        ],
        compiler_params=pltpu.CompilerParams(
            collective_id=0, has_side_effects=True, vmem_limit_bytes=58 * 2**20
        ),
        cost_estimate=pl.CostEstimate(
            flops=12 * wide * n_pb * chunk * dim,
            bytes_accessed=4 * rows * width * 2,
            transcendentals=wide * n_pb * chunk,
        ),
    )(block_mask, queries, keys, values, dout)
    return pl.pallas_call(
        hand_over,
        out_shape=tuple(jax.ShapeDtypeStruct(one.shape, one.dtype) for one in results),
        in_specs=[pl.BlockSpec(memory_space=pl.ANY)] * 4,
        out_specs=[pl.BlockSpec(memory_space=pltpu.VMEM)] * 4,
        scratch_shapes=[dma((4,))],
        compiler_params=pltpu.CompilerParams(vmem_limit_bytes=63 * 2**20),
    )(*results)


def solution(mesh):
    in_specs = (
        P("pb", None),
        P(("ka", "pb"), None),
        P(("ka", "pb"), None),
        P("pb", None),
        P("pb", "ka"),
    )
    out_specs = (P("pb", "ka"), P("pb", "ka"), P(("ka", "pb"), None), P(("ka", "pb"), None))
    return jax.shard_map(
        functools.partial(per_device, mesh.shape["pb"], mesh.shape["ka"]),
        mesh=mesh, in_specs=in_specs, out_specs=out_specs, check_vma=False,
    )
```

```python
import functools
import math

import jax
import jax.numpy as jnp
from jax import lax
from jax.experimental import pallas as pl
from jax.experimental.pallas import tpu as pltpu
from jax.sharding import PartitionSpec as P

BLOCK = 128
DEAD = 1e30
F32 = jnp.float32
BF16 = jnp.bfloat16


def dot_nn(a, b):
    return jnp.dot(a, b, preferred_element_type=F32)


def dot_nt(a, b):
    return lax.dot_general(a, b, (((1,), (1,)), ((), ())), preferred_element_type=F32)


def kernel(
    n_pb, n_ka,
    mask_ref, q_ref, k_ref, v_ref, do_ref,
    att_ref, qg_ref, kg_ref, vg_ref,
    kv, k_turned, q_rows, do_rows, q_turned, do_turned, weights, wide_scores, probs, dscores,
    out_acc, dq_acc, run_max, run_total, group_max, row_lse, row_delta,
    stat_recv, out_send, out_recv, dq_send, dq_recv,
    acc, core_send, core_recv, x_send, x_recv, z_send, z_recv,
    load_sem, ag_recv_sem, ag_z_sem, ag_x_sem, ag_core_sem,
    stat_send_sem, stat_recv_sem, out_send_sem, out_recv_sem, dq_send_sem, dq_recv_sem,
    core_send_sem, core_recv_sem, x_send_sem, x_recv_sem, z_send_sem, z_recv_sem,
):
    rows, width = q_ref.shape
    chunk, dim = k_ref.shape
    heads = width // dim
    own_heads = heads // n_ka
    groups = n_pb // 4
    group_keys = 4 * chunk
    group_blocks = group_keys // BLOCK
    scale = 1.0 / math.sqrt(dim)
    log_scale = scale * math.log2(math.e)

    me = lax.axis_index("pb")
    panel = lax.axis_index("ka")
    core = lax.rem(me, 2)
    x = lax.rem(me // 2, 2)
    z = me // 4
    other_core, other_x = 1 - core, 1 - x

    def at(z_index, x_index, core_index):
        return (z_index * 2 + x_index) * 2 + core_index

    core_peer, x_peer = at(z, x, other_core), at(z, other_x, core)

    def remote(src, dst, send_sem, recv_sem, device):
        return pltpu.make_async_remote_copy(
            src_ref=src, dst_ref=dst, send_sem=send_sem, recv_sem=recv_sem,
            device_id=device, device_id_type=pl.DeviceIdType.MESH,
        )

    def ring(start, step, size):
        return lax.rem(start + step, size)

    def load(index, src, dst):
        return pltpu.make_async_copy(src, dst, load_sem.at[index])

    loads = [
        load(0, k_ref, kv.at[me, pl.ds(0, chunk)]),
        load(1, v_ref, kv.at[me, pl.ds(chunk, chunk)]),
    ]
    for part, (src, dst) in enumerate(((q_ref, q_rows), (do_ref, do_rows))):
        for head in range(heads):
            loads.append(
                load(
                    2 + part * heads + head,
                    src.at[:, pl.ds(head * dim, dim)],
                    dst.at[pl.ds(head * rows, rows), :],
                )
            )
    for one in loads:
        one.start()

    barrier = pltpu.get_barrier_semaphore()
    partners = [{"pb": core_peer}, {"pb": x_peer}]
    partners += [{"pb": at(ring(z, s, groups), x, core)} for s in range(1, groups)]
    partners += [{"ka": ring(panel, s, n_ka)} for s in range(1, n_ka)]
    for partner in partners:
        pl.semaphore_signal(barrier, inc=1, device_id=partner, device_id_type=pl.DeviceIdType.MESH)
    loads[0].wait()
    loads[1].wait()
    pl.semaphore_wait(barrier, len(partners))

    def gather_copy(index, send_sem, device):
        return remote(kv.at[index], kv.at[index], send_sem, ag_recv_sem.at[index], {"pb": device})

    def z_copy(s):
        return gather_copy(me, ag_z_sem.at[s], at(ring(z, s, groups), x, core))

    def x_copy(k):
        return gather_copy(at(ring(z, k, groups), x, core), ag_x_sem.at[k], x_peer)

    def core_copy(k, part):
        owner_x = x if part == 0 else other_x
        index = at(ring(z, k, groups), owner_x, core)
        return gather_copy(index, ag_core_sem.at[2 * k + part], core_peer)

    def arrived(index):
        gather_copy(index, ag_x_sem.at[0], core_peer).wait_recv()

    x_copy(0).start()
    core_copy(0, 0).start()
    for s in range(1, groups):
        z_copy(s).start()

    def head_columns(head, count=1):
        return pl.ds(pl.multiple_of(head * rows, rows), count * rows)

    def head_at(i):
        return lax.rem((panel + 1) * own_heads + i, heads) if own_heads % 2 == 0 else i

    def foreign(head):
        return head // own_heads != panel

    out_acc[...] = jnp.zeros_like(out_acc)
    dq_acc[...] = jnp.zeros_like(dq_acc)
    run_max[...] = jnp.full_like(run_max, -1e38)
    run_total[...] = jnp.zeros_like(run_total)

    def stage_x(k):
        arrived(at(ring(z, k, groups), other_x, core))
        core_copy(k, 1).start()

    def stage_core(k):
        arrived(at(ring(z, k, groups), x, other_core))
        arrived(at(ring(z, k, groups), other_x, other_core))

    def turn(src, dst, first):
        for head in range(heads):
            loads[first + head].wait()
            span = pl.ds(head * rows, rows)
            dst[:, span] = src[span, :].T

    turn(q_rows, q_turned, 2)
    stage_x(0)
    turn(do_rows, do_turned, 2 + heads)
    stage_core(0)

    def group_rows(group, first):
        return kv[pl.ds(group * 4, 4), first : first + chunk, :].reshape(group_keys, dim)

    def stage_z(k):
        arrived(at(ring(z, k, groups), x, core))
        x_copy(k).start()
        core_copy(k, 0).start()

    def forward_group(k, middle=None):
        group = ring(z, k, groups)
        keys = group_rows(group, 0)
        k_turned[group] = keys.T
        values_turned = jnp.concatenate(
            [group_rows(group, chunk).T, jnp.ones((16, group_keys), BF16)], axis=0
        )
        bias = [
            (mask_ref[0, group * group_blocks + b].astype(F32) - 1.0) * DEAD
            for b in range(group_blocks)
        ]

        def forward_heads(first, last):
            def score(i):
                scores = dot_nn(group_rows(group, 0), q_turned[:, head_columns(head_at(i), 2)])
                wide_scores[(i - first) // 2] = scores
                return [
                    jnp.max(scores[b * BLOCK : (b + 1) * BLOCK], axis=0, keepdims=True) * log_scale
                    for b in range(group_blocks)
                ]

            peaks = score(first)
            for i in range(first, last, 2):
                later = score(i + 2) if i + 2 < last else None
                cols = head_columns(head_at(i), 2)
                peak = functools.reduce(jnp.maximum, [p + one for p, one in zip(peaks, bias)])
                low = []
                for b in range(group_blocks):
                    shift = jnp.maximum(peak - bias[b], peaks[b])
                    part = wide_scores[(i - first) // 2, b * BLOCK : (b + 1) * BLOCK, :]
                    low.append(jnp.exp2((part * log_scale - shift).astype(BF16)))
                low = jnp.concatenate(low, axis=0)
                weights[group, :, cols] = low
                group_max[group, :, cols] = peak
                old = run_max[:, cols]
                new = jnp.maximum(old, peak)
                keep, add = jnp.exp2(old - new), jnp.exp2(peak - new)
                run_max[:, cols] = new
                product = dot_nn(values_turned, low)
                total = product[dim : dim + 1]
                run_total[:, cols] = run_total[:, cols] * keep + total * add
                out_acc[:, cols] = out_acc[:, cols] * keep + product[0:dim] * add
                peaks = later

        if middle is None:
            forward_heads(0, heads)
        else:
            forward_heads(0, heads // 2)
            middle()
            forward_heads(heads // 2, heads)

    def later_group(k, _):
        @pl.when(k + 2 < groups)
        def _():
            stage_z(k + 2)

        @pl.when(k + 1 < groups)
        def _():
            stage_x(k + 1)

        forward_group(k)

        @pl.when(k + 1 < groups)
        def _():
            stage_core(k + 1)

        return 0

    def first_middle():
        stage_x(1)
        if groups > 2:
            stage_z(2)

    if groups > 1:
        stage_z(1)
        forward_group(0, first_middle)
        stage_core(1)
        lax.fori_loop(1, groups, later_group, 0)
    else:
        forward_group(0)

    def stat_copy(s):
        return remote(
            stat_recv.at[panel], stat_recv.at[panel],
            stat_send_sem.at[s], stat_recv_sem.at[panel], {"ka": ring(panel, s, n_ka)},
        )

    def stat_arrived(source):
        remote(
            stat_recv.at[source], stat_recv.at[source],
            stat_send_sem.at[0], stat_recv_sem.at[source], {"ka": ring(panel, 1, n_ka)},
        ).wait_recv()

    def part_copy(send, recv, send_sem, recv_sem, head):
        local = lax.rem(head, own_heads)
        return remote(
            send.at[head], recv.at[panel, local], send_sem.at[head], recv_sem.at[panel, local],
            {"ka": head // own_heads},
        )

    def part_arrived(recv, send_sem, recv_sem, source, local):
        remote(
            recv.at[source, local], recv.at[source, local],
            send_sem.at[0], recv_sem.at[source, local], {"ka": ring(panel, 1, n_ka)},
        ).wait_recv()

    totals = run_total[...]
    deltas = jnp.sum(out_acc[...] * do_turned[...].astype(F32), axis=0, keepdims=True)
    stat_recv[panel, 0:1, :] = run_max[...] + jnp.log2(totals)
    stat_recv[panel, 1:2, :] = deltas / totals
    for s in range(1, n_ka):
        stat_copy(s).start()

    def finish_out(i, _):
        head = head_at(i)
        cols = head_columns(head)
        out = (out_acc[:, cols] * (1.0 / run_total[:, cols])).astype(BF16)

        @pl.when(foreign(head))
        def _():
            out_send[head] = out
            part_copy(out_send, out_recv, out_send_sem, out_recv_sem, head).start()

        @pl.when(jnp.logical_not(foreign(head)))
        def _():
            out_recv[panel, lax.rem(head, own_heads)] = out

        return 0

    lax.fori_loop(0, heads, finish_out, 0, unroll=2)

    for s in range(1, n_ka):
        stat_arrived(ring(panel, s, n_ka))
    lses = [stat_recv[n, 0:1, :] for n in range(n_ka)]
    peak = functools.reduce(jnp.maximum, lses)
    lse = peak + jnp.log2(sum(jnp.exp2(one - peak) for one in lses))
    row_lse[...] = lse
    row_delta[...] = sum(jnp.exp2(lses[n] - lse) * stat_recv[n, 1:2, :] for n in range(n_ka))
    half = heads // 2

    def back_group_of(k):
        return ring(z, k + 1, groups)

    def core_sum_copy(k):
        return remote(
            core_send.at[k], core_recv.at[k], core_send_sem.at[k], core_recv_sem.at[k],
            {"pb": core_peer},
        )

    def x_sum_copy(k):
        return remote(
            x_send.at[k], x_recv.at[k], x_send_sem.at[k], x_recv_sem.at[k], {"pb": x_peer}
        )

    def z_sum_copy(k):
        return remote(
            z_send.at[k], z_recv.at[k], z_send_sem.at[k], z_recv_sem.at[k],
            {"pb": at(back_group_of(k), x, core)},
        )

    def send_core(k):
        for part in range(2):
            core_send[k, part] = acc[k, 2 * part + other_core].astype(BF16)
        core_sum_copy(k).start()

    def send_x(k):
        core_sum_copy(k).wait_recv()
        passed = acc[k, 2 * other_x + core] + core_recv[k, other_x].astype(F32)
        x_send[k] = passed.astype(BF16)
        x_sum_copy(k).start()
        mine = 2 * x + core
        acc[k, mine] = acc[k, mine] + core_recv[k, x].astype(F32)

    def x_total(k):
        x_sum_copy(k).wait_recv()
        return acc[k, 2 * x + core] + x_recv[k].astype(F32)

    def send_z(k):
        z_send[k] = x_total(k).astype(BF16)
        z_sum_copy(k).start()

    def backward_block(k, first, last, middle=lambda: None):
        group = back_group_of(k)
        sums = []

        def rows_of(i):
            return pl.ds(pl.multiple_of(head_at(i) * rows, rows), 2 * rows)

        def products(i):
            cols = head_columns(head_at(i), 2)
            place = slice(i * rows, (i + 2) * rows)
            dq_acc[:, cols] = dq_acc[:, cols] + dot_nn(k_turned[group], dscores[:, place])
            sums.append(
                (
                    dot_nn(dscores[:, place], q_rows[rows_of(i), :]),
                    dot_nn(probs[:, place], do_rows[rows_of(i), :]),
                )
            )

        for i in range(first, last, 2):
            cols = head_columns(head_at(i), 2)
            place = slice(i * rows, (i + 2) * rows)
            mix = jnp.exp2(group_max[group, :, cols] - row_lse[:, cols])
            dprobs = dot_nn(group_rows(group, chunk), do_turned[:, cols])
            if i > first:
                products(i - 2)
            low = weights[group, :, cols] * mix.astype(BF16)
            probs[:, place] = low
            dscores[:, place] = low * (dprobs - row_delta[:, cols]).astype(BF16)
        middle()
        products(last - 2)
        key_part = sum(one[0] for one in sums) * scale
        value_part = sum(one[1] for one in sums)
        return key_part.reshape(4, chunk, dim), value_part.reshape(4, chunk, dim)

    def send_dq(i, _):
        head = head_at(i)

        @pl.when(foreign(head))
        def _():
            dq_send[head] = (dq_acc[:, head_columns(head)] * scale).astype(BF16)
            part_copy(dq_send, dq_recv, dq_send_sem, dq_recv_sem, head).start()

        return 0

    def sweep_one(k, _):
        key_part, value_part = backward_block(k, 0, half)
        acc[k, :, 0:chunk, :] = key_part
        acc[k, :, chunk : 2 * chunk, :] = value_part
        return 0

    def sweep_two(k, _):
        def middle():
            @pl.when(k > 0)
            def _():
                send_x(k - 1)

            @pl.when(k > 1)
            def _():
                send_z(k - 2)

        key_part, value_part = backward_block(k, half, heads, middle)
        acc[k, :, 0:chunk, :] = acc[k, :, 0:chunk, :] + key_part
        acc[k, :, chunk : 2 * chunk, :] = acc[k, :, chunk : 2 * chunk, :] + value_part
        send_core(k)
        return 0

    lax.fori_loop(0, groups, sweep_one, 0, unroll=2)
    lax.fori_loop(0, half, send_dq, 0)
    lax.fori_loop(0, groups, sweep_two, 0)
    lax.fori_loop(half, heads, send_dq, 0)
    last = groups - 1
    if groups > 1:
        send_z(last - 1)
    send_x(last)

    for local in range(own_heads):
        head = panel * own_heads + local
        cols = head_columns(head)
        for s in range(1, n_ka):
            part_arrived(out_recv, out_send_sem, out_recv_sem, ring(panel, s, n_ka), local)
        lse = row_lse[:, cols]
        mixed = sum(
            jnp.exp2(stat_recv[n, 0:1, cols] - lse) * out_recv[n, local].astype(F32)
            for n in range(n_ka)
        )
        att_ref[:, local * dim : (local + 1) * dim] = mixed.T.astype(BF16)
        dq_recv[panel, local] = (dq_acc[:, cols] * scale).astype(BF16)

    for local in range(own_heads):
        for s in range(1, n_ka):
            part_arrived(dq_recv, dq_send_sem, dq_recv_sem, ring(panel, s, n_ka), local)
        summed = sum(dq_recv[n, local].astype(F32) for n in range(n_ka))
        qg_ref[:, local * dim : (local + 1) * dim] = summed.T

    total = x_total(last)
    for k in range(last):
        z_sum_copy(k).wait_recv()
        total = total + z_recv[k].astype(F32)
    kg_ref[...] = total[0:chunk]
    vg_ref[...] = total[chunk : 2 * chunk]

    def drain_group(k, _):
        x_copy(k).wait_send()
        core_copy(k, 0).wait_send()
        core_copy(k, 1).wait_send()
        core_sum_copy(k).wait_send()
        x_sum_copy(k).wait_send()

        @pl.when(k < last)
        def _():
            z_copy(k + 1).wait_send()
            z_sum_copy(k).wait_send()

        return 0

    lax.fori_loop(0, groups, drain_group, 0)

    def drain_head(i, _):
        head = head_at(i)
        @pl.when(foreign(head))
        def _():
            part_copy(out_send, out_recv, out_send_sem, out_recv_sem, head).wait_send()
            part_copy(dq_send, dq_recv, dq_send_sem, dq_recv_sem, head).wait_send()

        return 0

    lax.fori_loop(0, heads, drain_head, 0)
    for s in range(1, n_ka):
        stat_copy(s).wait_send()


def hand_over(*refs):
    sources, targets, stops, read_sem, write_sem = refs[:4], refs[4:8], refs[8:12], refs[12], refs[13]
    order = (2, 3, 0, 1)
    reads = [pltpu.make_async_copy(sources[i], stops[i], read_sem.at[i]) for i in range(4)]
    writes = [pltpu.make_async_copy(stops[i], targets[i], write_sem.at[i]) for i in range(4)]
    for i in order:
        reads[i].start()
    for i in order:
        reads[i].wait()
        writes[i].start()
    for i in order:
        writes[i].wait()


def per_device(n_pb, n_ka, queries, keys, values, dout, block_mask):
    rows, width = queries.shape
    chunk, dim = keys.shape
    heads = width // dim
    own_heads = heads // n_ka
    groups = n_pb // 4
    group_keys = 4 * chunk
    wide = heads * rows
    assert rows == 2 * BLOCK and heads % 4 == 0 and group_keys % BLOCK == 0
    vmem, dma = pltpu.VMEM, pltpu.SemaphoreType.DMA
    pair = (2 * chunk, dim)
    results = pl.pallas_call(
        functools.partial(kernel, n_pb, n_ka),
        out_shape=(
            jax.ShapeDtypeStruct((rows, own_heads * dim), BF16),
            jax.ShapeDtypeStruct((rows, own_heads * dim), F32),
            jax.ShapeDtypeStruct((chunk, dim), F32),
            jax.ShapeDtypeStruct((chunk, dim), F32),
        ),
        in_specs=[pl.BlockSpec(memory_space=pltpu.SMEM)]
        + [pl.BlockSpec(memory_space=pl.ANY)] * 4,
        out_specs=[pl.BlockSpec(memory_space=pltpu.VMEM)] * 4,
        scratch_shapes=[
            vmem((n_pb,) + pair, BF16),
            vmem((groups, dim, group_keys), BF16),
            vmem((wide, dim), BF16),
            vmem((wide, dim), BF16),
            vmem((dim, wide), BF16),
            vmem((dim, wide), BF16),
            vmem((groups, group_keys, wide), BF16),
            vmem((heads // 2, group_keys, 2 * rows), F32),
            vmem((group_keys, wide), BF16),
            vmem((group_keys, wide), BF16),
            vmem((dim, wide), F32),
            vmem((dim, wide), F32),
            vmem((1, wide), F32),
            vmem((1, wide), F32),
            vmem((groups, 1, wide), F32),
            vmem((1, wide), F32),
            vmem((1, wide), F32),
            vmem((n_ka, 2, wide), F32),
            vmem((heads, dim, rows), BF16),
            vmem((n_ka, own_heads, dim, rows), BF16),
            vmem((heads, dim, rows), BF16),
            vmem((n_ka, own_heads, dim, rows), BF16),
            vmem((groups, 4) + pair, F32),
            vmem((groups, 2) + pair, BF16),
            vmem((groups, 2) + pair, BF16),
            vmem((groups,) + pair, BF16),
            vmem((groups,) + pair, BF16),
            vmem((groups,) + pair, BF16),
            vmem((groups,) + pair, BF16),
            dma((2 + 2 * heads,)),
            dma((n_pb,)),
            dma((groups,)),
            dma((groups,)),
            dma((2 * groups,)),
            dma((n_ka,)),
            dma((n_ka,)),
            dma((heads,)),
            dma((n_ka, own_heads)),
            dma((heads,)),
            dma((n_ka, own_heads)),
            dma((groups,)),
            dma((groups,)),
            dma((groups,)),
            dma((groups,)),
            dma((groups,)),
            dma((groups,)),
        ],
        compiler_params=pltpu.CompilerParams(
            collective_id=0, has_side_effects=True, vmem_limit_bytes=58 * 2**20
        ),
        cost_estimate=pl.CostEstimate(
            flops=12 * wide * n_pb * chunk * dim,
            bytes_accessed=4 * rows * width * 2,
            transcendentals=wide * n_pb * chunk,
        ),
    )(block_mask, queries, keys, values, dout)
    return pl.pallas_call(
        hand_over,
        out_shape=tuple(jax.ShapeDtypeStruct(one.shape, one.dtype) for one in results),
        in_specs=[pl.BlockSpec(memory_space=pl.ANY)] * 4,
        out_specs=[pl.BlockSpec(memory_space=pl.ANY)] * 4,
        scratch_shapes=[vmem(one.shape, one.dtype) for one in results] + [dma((4,))] * 2,
        compiler_params=pltpu.CompilerParams(vmem_limit_bytes=63 * 2**20),
    )(*results)


def solution(mesh):
    in_specs = (
        P("pb", None),
        P(("ka", "pb"), None),
        P(("ka", "pb"), None),
        P("pb", None),
        P("pb", "ka"),
    )
    out_specs = (P("pb", "ka"), P("pb", "ka"), P(("ka", "pb"), None), P(("ka", "pb"), None))
    return jax.shard_map(
        functools.partial(per_device, mesh.shape["pb"], mesh.shape["ka"]),
        mesh=mesh, in_specs=in_specs, out_specs=out_specs, check_vma=False,
    )
```

```python
import functools
import math

import jax
import jax.numpy as jnp
from jax import lax
from jax.experimental import pallas as pl
from jax.experimental.pallas import tpu as pltpu
from jax.sharding import PartitionSpec as P

BLOCK = 128
DEAD = 1e30
F32 = jnp.float32
BF16 = jnp.bfloat16


def dot_nn(a, b):
    return jnp.dot(a, b, preferred_element_type=F32)


def dot_nt(a, b):
    return lax.dot_general(a, b, (((1,), (1,)), ((), ())), preferred_element_type=F32)


def kernel(
    n_pb, n_ka,
    mask_ref, q_ref, k_ref, v_ref, do_ref,
    att_ref, qg_ref, kg_ref, vg_ref,
    kv, k_turned, q_rows, do_rows, q_turned, do_turned, weights, wide_scores, probs, dscores,
    out_acc, dq_acc, run_max, run_total, group_max, row_lse, row_delta,
    stat_recv, out_send, out_recv, dq_send, dq_recv,
    acc, core_send, core_recv, x_send, x_recv, z_send, z_recv,
    load_sem, ag_recv_sem, ag_z_sem, ag_x_sem, ag_core_sem,
    stat_send_sem, stat_recv_sem, out_send_sem, out_recv_sem, dq_send_sem, dq_recv_sem,
    core_send_sem, core_recv_sem, x_send_sem, x_recv_sem, z_send_sem, z_recv_sem,
):
    rows, width = q_ref.shape
    chunk, dim = k_ref.shape
    heads = width // dim
    own_heads = heads // n_ka
    groups = n_pb // 4
    group_keys = 4 * chunk
    group_blocks = group_keys // BLOCK
    scale = 1.0 / math.sqrt(dim)
    log_scale = scale * math.log2(math.e)

    me = lax.axis_index("pb")
    panel = lax.axis_index("ka")
    core = lax.rem(me, 2)
    x = lax.rem(me // 2, 2)
    z = me // 4
    other_core, other_x = 1 - core, 1 - x

    def at(z_index, x_index, core_index):
        return (z_index * 2 + x_index) * 2 + core_index

    core_peer, x_peer = at(z, x, other_core), at(z, other_x, core)

    def remote(src, dst, send_sem, recv_sem, device):
        return pltpu.make_async_remote_copy(
            src_ref=src, dst_ref=dst, send_sem=send_sem, recv_sem=recv_sem,
            device_id=device, device_id_type=pl.DeviceIdType.MESH,
        )

    def ring(start, step, size):
        return lax.rem(start + step, size)

    def load(index, src, dst):
        return pltpu.make_async_copy(src, dst, load_sem.at[index])

    loads = [
        load(0, k_ref, kv.at[me, pl.ds(0, chunk)]),
        load(1, v_ref, kv.at[me, pl.ds(chunk, chunk)]),
    ]
    for part, (src, dst) in enumerate(((q_ref, q_rows), (do_ref, do_rows))):
        for head in range(heads):
            loads.append(
                load(
                    2 + part * heads + head,
                    src.at[:, pl.ds(head * dim, dim)],
                    dst.at[pl.ds(head * rows, rows), :],
                )
            )
    for one in loads:
        one.start()

    barrier = pltpu.get_barrier_semaphore()
    partners = [{"pb": core_peer}, {"pb": x_peer}]
    partners += [{"pb": at(ring(z, s, groups), x, core)} for s in range(1, groups)]
    partners += [{"ka": ring(panel, s, n_ka)} for s in range(1, n_ka)]
    for partner in partners:
        pl.semaphore_signal(barrier, inc=1, device_id=partner, device_id_type=pl.DeviceIdType.MESH)
    loads[0].wait()
    loads[1].wait()
    pl.semaphore_wait(barrier, len(partners))

    def gather_copy(index, send_sem, device):
        return remote(kv.at[index], kv.at[index], send_sem, ag_recv_sem.at[index], {"pb": device})

    def z_copy(s):
        return gather_copy(me, ag_z_sem.at[s], at(ring(z, s, groups), x, core))

    def x_copy(k):
        return gather_copy(at(ring(z, k, groups), x, core), ag_x_sem.at[k], x_peer)

    def core_copy(k, part):
        owner_x = x if part == 0 else other_x
        index = at(ring(z, k, groups), owner_x, core)
        return gather_copy(index, ag_core_sem.at[2 * k + part], core_peer)

    def arrived(index):
        gather_copy(index, ag_x_sem.at[0], core_peer).wait_recv()

    x_copy(0).start()
    core_copy(0, 0).start()
    for s in range(1, groups):
        z_copy(s).start()

    def head_columns(head, count=1):
        return pl.ds(pl.multiple_of(head * rows, rows), count * rows)

    def head_at(i):
        return lax.rem((panel + 1) * own_heads + i, heads) if own_heads % 2 == 0 else i

    def foreign(head):
        return head // own_heads != panel

    out_acc[...] = jnp.zeros_like(out_acc)
    dq_acc[...] = jnp.zeros_like(dq_acc)
    run_max[...] = jnp.full_like(run_max, -1e38)
    run_total[...] = jnp.zeros_like(run_total)

    def stage_x(k):
        arrived(at(ring(z, k, groups), other_x, core))
        core_copy(k, 1).start()

    def stage_core(k):
        arrived(at(ring(z, k, groups), x, other_core))
        arrived(at(ring(z, k, groups), other_x, other_core))

    def turn(src, dst, first):
        for head in range(heads):
            loads[first + head].wait()
            span = pl.ds(head * rows, rows)
            dst[:, span] = src[span, :].T

    turn(q_rows, q_turned, 2)
    stage_x(0)
    turn(do_rows, do_turned, 2 + heads)
    stage_core(0)

    def group_rows(group, first):
        return kv[pl.ds(group * 4, 4), first : first + chunk, :].reshape(group_keys, dim)

    def stage_z(k):
        arrived(at(ring(z, k, groups), x, core))
        x_copy(k).start()
        core_copy(k, 0).start()

    def forward_group(k, middle=None):
        group = ring(z, k, groups)
        keys = group_rows(group, 0)
        k_turned[group] = keys.T
        values_turned = jnp.concatenate(
            [group_rows(group, chunk).T, jnp.ones((16, group_keys), BF16)], axis=0
        )
        bias = [
            (mask_ref[0, group * group_blocks + b].astype(F32) - 1.0) * DEAD
            for b in range(group_blocks)
        ]

        def forward_heads(first, last):
            def score(i):
                scores = dot_nn(group_rows(group, 0), q_turned[:, head_columns(head_at(i), 2)])
                wide_scores[(i - first) // 2] = scores
                return [
                    jnp.max(scores[b * BLOCK : (b + 1) * BLOCK], axis=0, keepdims=True) * log_scale
                    for b in range(group_blocks)
                ]

            peaks = score(first)
            for i in range(first, last, 2):
                later = score(i + 2) if i + 2 < last else None
                cols = head_columns(head_at(i), 2)
                peak = functools.reduce(jnp.maximum, [p + one for p, one in zip(peaks, bias)])
                low = []
                for b in range(group_blocks):
                    shift = jnp.maximum(peak - bias[b], peaks[b])
                    part = wide_scores[(i - first) // 2, b * BLOCK : (b + 1) * BLOCK, :]
                    low.append(jnp.exp2(part * log_scale - shift).astype(BF16))
                low = jnp.concatenate(low, axis=0)
                weights[group, :, cols] = low
                group_max[group, :, cols] = peak
                old = run_max[:, cols]
                new = jnp.maximum(old, peak)
                keep, add = jnp.exp2(old - new), jnp.exp2(peak - new)
                run_max[:, cols] = new
                product = dot_nn(values_turned, low)
                total = product[dim : dim + 1]
                run_total[:, cols] = run_total[:, cols] * keep + total * add
                out_acc[:, cols] = out_acc[:, cols] * keep + product[0:dim] * add
                peaks = later

        if middle is None:
            forward_heads(0, heads)
        else:
            forward_heads(0, heads // 2)
            middle()
            forward_heads(heads // 2, heads)

    def later_group(k, _):
        @pl.when(k + 2 < groups)
        def _():
            stage_z(k + 2)

        @pl.when(k + 1 < groups)
        def _():
            stage_x(k + 1)

        forward_group(k)

        @pl.when(k + 1 < groups)
        def _():
            stage_core(k + 1)

        return 0

    def first_middle():
        stage_x(1)
        if groups > 2:
            stage_z(2)

    if groups > 1:
        stage_z(1)
        forward_group(0, first_middle)
        stage_core(1)
        lax.fori_loop(1, groups, later_group, 0)
    else:
        forward_group(0)

    def stat_copy(s):
        return remote(
            stat_recv.at[panel], stat_recv.at[panel],
            stat_send_sem.at[s], stat_recv_sem.at[panel], {"ka": ring(panel, s, n_ka)},
        )

    def stat_arrived(source):
        remote(
            stat_recv.at[source], stat_recv.at[source],
            stat_send_sem.at[0], stat_recv_sem.at[source], {"ka": ring(panel, 1, n_ka)},
        ).wait_recv()

    def part_copy(send, recv, send_sem, recv_sem, head):
        local = lax.rem(head, own_heads)
        return remote(
            send.at[head], recv.at[panel, local], send_sem.at[head], recv_sem.at[panel, local],
            {"ka": head // own_heads},
        )

    def part_arrived(recv, send_sem, recv_sem, source, local):
        remote(
            recv.at[source, local], recv.at[source, local],
            send_sem.at[0], recv_sem.at[source, local], {"ka": ring(panel, 1, n_ka)},
        ).wait_recv()

    totals = run_total[...]
    deltas = jnp.sum(out_acc[...] * do_turned[...].astype(F32), axis=0, keepdims=True)
    stat_recv[panel, 0:1, :] = run_max[...] + jnp.log2(totals)
    stat_recv[panel, 1:2, :] = deltas / totals
    for s in range(1, n_ka):
        stat_copy(s).start()

    def finish_out(i, _):
        head = head_at(i)
        cols = head_columns(head)
        out = (out_acc[:, cols] * (1.0 / run_total[:, cols])).astype(BF16)

        @pl.when(foreign(head))
        def _():
            out_send[head] = out
            part_copy(out_send, out_recv, out_send_sem, out_recv_sem, head).start()

        @pl.when(jnp.logical_not(foreign(head)))
        def _():
            out_recv[panel, lax.rem(head, own_heads)] = out

        return 0

    lax.fori_loop(0, heads, finish_out, 0, unroll=2)

    for s in range(1, n_ka):
        stat_arrived(ring(panel, s, n_ka))
    lses = [stat_recv[n, 0:1, :] for n in range(n_ka)]
    peak = functools.reduce(jnp.maximum, lses)
    lse = peak + jnp.log2(sum(jnp.exp2(one - peak) for one in lses))
    row_lse[...] = lse
    row_delta[...] = sum(jnp.exp2(lses[n] - lse) * stat_recv[n, 1:2, :] for n in range(n_ka))
    half = heads // 2

    def back_group_of(k):
        return ring(z, k + 1, groups)

    def core_sum_copy(k):
        return remote(
            core_send.at[k], core_recv.at[k], core_send_sem.at[k], core_recv_sem.at[k],
            {"pb": core_peer},
        )

    def x_sum_copy(k):
        return remote(
            x_send.at[k], x_recv.at[k], x_send_sem.at[k], x_recv_sem.at[k], {"pb": x_peer}
        )

    def z_sum_copy(k):
        return remote(
            z_send.at[k], z_recv.at[k], z_send_sem.at[k], z_recv_sem.at[k],
            {"pb": at(back_group_of(k), x, core)},
        )

    def send_core(k):
        for part in range(2):
            core_send[k, part] = acc[k, 2 * part + other_core].astype(BF16)
        core_sum_copy(k).start()

    def send_x(k):
        core_sum_copy(k).wait_recv()
        passed = acc[k, 2 * other_x + core] + core_recv[k, other_x].astype(F32)
        x_send[k] = passed.astype(BF16)
        x_sum_copy(k).start()
        mine = 2 * x + core
        acc[k, mine] = acc[k, mine] + core_recv[k, x].astype(F32)

    def x_total(k):
        x_sum_copy(k).wait_recv()
        return acc[k, 2 * x + core] + x_recv[k].astype(F32)

    def send_z(k):
        z_send[k] = x_total(k).astype(BF16)
        z_sum_copy(k).start()

    def backward_block(k, first, last, middle=lambda: None):
        group = back_group_of(k)
        sums = []

        def rows_of(i):
            return pl.ds(pl.multiple_of(head_at(i) * rows, rows), 2 * rows)

        def products(i):
            cols = head_columns(head_at(i), 2)
            place = slice(i * rows, (i + 2) * rows)
            dq_acc[:, cols] = dq_acc[:, cols] + dot_nn(k_turned[group], dscores[:, place])
            sums.append(
                (
                    dot_nn(dscores[:, place], q_rows[rows_of(i), :]),
                    dot_nn(probs[:, place], do_rows[rows_of(i), :]),
                )
            )

        for i in range(first, last, 2):
            cols = head_columns(head_at(i), 2)
            place = slice(i * rows, (i + 2) * rows)
            mix = jnp.exp2(group_max[group, :, cols] - row_lse[:, cols])
            dprobs = dot_nn(group_rows(group, chunk), do_turned[:, cols])
            if i > first:
                products(i - 2)
            low = weights[group, :, cols] * mix.astype(BF16)
            probs[:, place] = low
            dscores[:, place] = low * (dprobs - row_delta[:, cols]).astype(BF16)
        middle()
        products(last - 2)
        key_part = sum(one[0] for one in sums) * scale
        value_part = sum(one[1] for one in sums)
        return key_part.reshape(4, chunk, dim), value_part.reshape(4, chunk, dim)

    def send_dq(i, _):
        head = head_at(i)

        @pl.when(foreign(head))
        def _():
            dq_send[head] = (dq_acc[:, head_columns(head)] * scale).astype(BF16)
            part_copy(dq_send, dq_recv, dq_send_sem, dq_recv_sem, head).start()

        return 0

    def sweep_one(k, _):
        key_part, value_part = backward_block(k, 0, half)
        acc[k, :, 0:chunk, :] = key_part
        acc[k, :, chunk : 2 * chunk, :] = value_part
        return 0

    def sweep_two(k, _):
        def middle():
            @pl.when(k > 0)
            def _():
                send_x(k - 1)

            @pl.when(k > 1)
            def _():
                send_z(k - 2)

        key_part, value_part = backward_block(k, half, heads, middle)
        acc[k, :, 0:chunk, :] = acc[k, :, 0:chunk, :] + key_part
        acc[k, :, chunk : 2 * chunk, :] = acc[k, :, chunk : 2 * chunk, :] + value_part
        send_core(k)
        return 0

    lax.fori_loop(0, groups, sweep_one, 0, unroll=4 if groups % 4 == 0 else 1)
    lax.fori_loop(0, half, send_dq, 0)
    lax.fori_loop(0, groups, sweep_two, 0)
    lax.fori_loop(half, heads, send_dq, 0)
    last = groups - 1
    if groups > 1:
        send_z(last - 1)
    send_x(last)

    for local in range(own_heads):
        head = panel * own_heads + local
        cols = head_columns(head)
        for s in range(1, n_ka):
            part_arrived(out_recv, out_send_sem, out_recv_sem, ring(panel, s, n_ka), local)
        lse = row_lse[:, cols]
        mixed = sum(
            jnp.exp2(stat_recv[n, 0:1, cols] - lse) * out_recv[n, local].astype(F32)
            for n in range(n_ka)
        )
        att_ref[:, local * dim : (local + 1) * dim] = mixed.T.astype(BF16)
        dq_recv[panel, local] = (dq_acc[:, cols] * scale).astype(BF16)

    for local in range(own_heads):
        for s in range(1, n_ka):
            part_arrived(dq_recv, dq_send_sem, dq_recv_sem, ring(panel, s, n_ka), local)
        summed = sum(dq_recv[n, local].astype(F32) for n in range(n_ka))
        qg_ref[:, local * dim : (local + 1) * dim] = summed.T

    total = x_total(last)
    for k in range(last):
        z_sum_copy(k).wait_recv()
        total = total + z_recv[k].astype(F32)
    kg_ref[...] = total[0:chunk]
    vg_ref[...] = total[chunk : 2 * chunk]

    def drain_group(k, _):
        x_copy(k).wait_send()
        core_copy(k, 0).wait_send()
        core_copy(k, 1).wait_send()
        core_sum_copy(k).wait_send()
        x_sum_copy(k).wait_send()

        @pl.when(k < last)
        def _():
            z_copy(k + 1).wait_send()
            z_sum_copy(k).wait_send()

        return 0

    lax.fori_loop(0, groups, drain_group, 0)

    def drain_head(i, _):
        head = head_at(i)
        @pl.when(foreign(head))
        def _():
            part_copy(out_send, out_recv, out_send_sem, out_recv_sem, head).wait_send()
            part_copy(dq_send, dq_recv, dq_send_sem, dq_recv_sem, head).wait_send()

        return 0

    lax.fori_loop(0, heads, drain_head, 0)
    for s in range(1, n_ka):
        stat_copy(s).wait_send()


def hand_over(*refs):
    sources, targets, stops, read_sem, write_sem = refs[:4], refs[4:8], refs[8:12], refs[12], refs[13]
    order = (2, 3, 0, 1)
    reads = [pltpu.make_async_copy(sources[i], stops[i], read_sem.at[i]) for i in range(4)]
    writes = [pltpu.make_async_copy(stops[i], targets[i], write_sem.at[i]) for i in range(4)]
    for i in order:
        reads[i].start()
    for i in order:
        reads[i].wait()
        writes[i].start()
    for i in order:
        writes[i].wait()


def per_device(n_pb, n_ka, queries, keys, values, dout, block_mask):
    rows, width = queries.shape
    chunk, dim = keys.shape
    heads = width // dim
    own_heads = heads // n_ka
    groups = n_pb // 4
    group_keys = 4 * chunk
    wide = heads * rows
    assert rows == 2 * BLOCK and heads % 4 == 0 and group_keys % BLOCK == 0
    vmem, dma = pltpu.VMEM, pltpu.SemaphoreType.DMA
    pair = (2 * chunk, dim)
    results = pl.pallas_call(
        functools.partial(kernel, n_pb, n_ka),
        out_shape=(
            jax.ShapeDtypeStruct((rows, own_heads * dim), BF16),
            jax.ShapeDtypeStruct((rows, own_heads * dim), F32),
            jax.ShapeDtypeStruct((chunk, dim), F32),
            jax.ShapeDtypeStruct((chunk, dim), F32),
        ),
        in_specs=[pl.BlockSpec(memory_space=pltpu.SMEM)]
        + [pl.BlockSpec(memory_space=pl.ANY)] * 4,
        out_specs=[pl.BlockSpec(memory_space=pltpu.VMEM)] * 4,
        scratch_shapes=[
            vmem((n_pb,) + pair, BF16),
            vmem((groups, dim, group_keys), BF16),
            vmem((wide, dim), BF16),
            vmem((wide, dim), BF16),
            vmem((dim, wide), BF16),
            vmem((dim, wide), BF16),
            vmem((groups, group_keys, wide), BF16),
            vmem((heads // 2, group_keys, 2 * rows), F32),
            vmem((group_keys, wide), BF16),
            vmem((group_keys, wide), BF16),
            vmem((dim, wide), F32),
            vmem((dim, wide), F32),
            vmem((1, wide), F32),
            vmem((1, wide), F32),
            vmem((groups, 1, wide), F32),
            vmem((1, wide), F32),
            vmem((1, wide), F32),
            vmem((n_ka, 2, wide), F32),
            vmem((heads, dim, rows), BF16),
            vmem((n_ka, own_heads, dim, rows), BF16),
            vmem((heads, dim, rows), BF16),
            vmem((n_ka, own_heads, dim, rows), BF16),
            vmem((groups, 4) + pair, F32),
            vmem((groups, 2) + pair, BF16),
            vmem((groups, 2) + pair, BF16),
            vmem((groups,) + pair, BF16),
            vmem((groups,) + pair, BF16),
            vmem((groups,) + pair, BF16),
            vmem((groups,) + pair, BF16),
            dma((2 + 2 * heads,)),
            dma((n_pb,)),
            dma((groups,)),
            dma((groups,)),
            dma((2 * groups,)),
            dma((n_ka,)),
            dma((n_ka,)),
            dma((heads,)),
            dma((n_ka, own_heads)),
            dma((heads,)),
            dma((n_ka, own_heads)),
            dma((groups,)),
            dma((groups,)),
            dma((groups,)),
            dma((groups,)),
            dma((groups,)),
            dma((groups,)),
        ],
        compiler_params=pltpu.CompilerParams(
            collective_id=0, has_side_effects=True, vmem_limit_bytes=58 * 2**20
        ),
        cost_estimate=pl.CostEstimate(
            flops=12 * wide * n_pb * chunk * dim,
            bytes_accessed=4 * rows * width * 2,
            transcendentals=wide * n_pb * chunk,
        ),
    )(block_mask, queries, keys, values, dout)
    return pl.pallas_call(
        hand_over,
        out_shape=tuple(jax.ShapeDtypeStruct(one.shape, one.dtype) for one in results),
        in_specs=[pl.BlockSpec(memory_space=pl.ANY)] * 4,
        out_specs=[pl.BlockSpec(memory_space=pl.ANY)] * 4,
        scratch_shapes=[vmem(one.shape, one.dtype) for one in results] + [dma((4,))] * 2,
        compiler_params=pltpu.CompilerParams(vmem_limit_bytes=63 * 2**20),
    )(*results)


def solution(mesh):
    in_specs = (
        P("pb", None),
        P(("ka", "pb"), None),
        P(("ka", "pb"), None),
        P("pb", None),
        P("pb", "ka"),
    )
    out_specs = (P("pb", "ka"), P("pb", "ka"), P(("ka", "pb"), None), P(("ka", "pb"), None))
    return jax.shard_map(
        functools.partial(per_device, mesh.shape["pb"], mesh.shape["ka"]),
        mesh=mesh, in_specs=in_specs, out_specs=out_specs, check_vma=False,
    )
```
